256 devices in a mesh: row: 4 (over z_hi), col: 16 (over z_lo, y, core), layer: 4 (over x).
Axes of the slice: x: 4, y: 4, z: 8 (z_hi: 4, z_lo: 2; z = z_hi * 2 + z_lo), core: 2. Of those that a mesh axis runs over, the one named last changes fastest.
Arguments:
- x_tiles: bfloat16 [8, 256, 2, 128, 128], P('layer', ('row', 'col')), may hold values from -1 to 1
- x_cols: int32 [8, 256, 2], P('layer', ('row', 'col')), may hold values from 0 to 511, as said below
- c_list: int32 [4, 16, 256, 2], P('row', 'col'), may hold values from 0 to 63, as said below
- c_count: int32 [4, 16], P('row', 'col'), may hold values from 1 to 256, as said below
Outputs:
- c_tiles: float32 [4, 16, 256, 128, 128], P('row', 'col', 'layer')
The draws below stay inside these ranges and needn't reach their ends.
Inputs may be any that keep to these rules, and one draw needn't show every extreme that they name: `x_cols`: inside one section the 2 column indices of a block row are distinct. `c_list`: the first entry indexes the 64 block rows of the grid row, the second the 16 block rows of the grid column; the slots of one grid position hold distinct pairs. `c_count`: some grid position has all 256 slots live in every draw.
All inputs are finite; a program needn't handle non-finite values.
Results may differ from the reference program's by a relative error of at most 0.011.
Values may be sent and summed in bfloat16 or wider, within the bound.
A program may use at most 128 MiB of HBM per device.

```python
import math
import jax
import jax.numpy as jnp
from jax import lax

TILE_EDGE = 128
SECTION_NNZ = 2
LOCAL_SECTIONS = 2
ROWS_DEV = 4
SECTIONS = 8
PANEL_COLS = 512
A_ROWS = 64
B_ROWS = 16
SLAB_ROWS = 256
C_SLOTS = 256
N_ROW = 4
N_COL = 16
N_LAYER = 4


def draw_x_cols(key, part):
    key = jax.random.fold_in(key, 11)
    base_key, pick_key = jax.random.split(key)
    window = 2 * SECTION_NNZ - 1
    bases = jax.random.randint(base_key, (SECTIONS, ROWS_DEV), 0, PANEL_COLS - window + 1)
    subkeys = jax.random.split(pick_key, SECTIONS * SLAB_ROWS)
    picks = jax.vmap(lambda subkey: jax.random.permutation(subkey, window)[:SECTION_NNZ])(subkeys)
    picks = picks.reshape(SECTIONS, SLAB_ROWS, SECTION_NNZ)
    row_kinds = jnp.arange(SLAB_ROWS) % ROWS_DEV
    return (bases[:, row_kinds][:, :, None] + picks).astype(jnp.int32)


def draw_c_list(key, part):
    key = jax.random.fold_in(key, 23)
    subkeys = jax.random.split(key, N_ROW * N_COL)
    orders = jax.vmap(lambda subkey: jax.random.permutation(subkey, C_SLOTS))(subkeys)
    kinds = orders % ROWS_DEV
    col_part = orders // ROWS_DEV % N_COL
    row_part = orders // (ROWS_DEV * N_COL)
    joined = jnp.stack([col_part * ROWS_DEV + kinds, row_part * ROWS_DEV + kinds], axis=-1)
    return joined.reshape(N_ROW, N_COL, C_SLOTS, 2).astype(jnp.int32)


def draw_c_count(key, part):
    key = jax.random.fold_in(key, 37)
    shift_key, cut_key, full_key = jax.random.split(key, 3)
    owners = N_ROW * N_COL
    shifts = jax.random.randint(shift_key, (owners,), 0, 4)
    levels = jnp.right_shift(jnp.full((owners,), C_SLOTS, jnp.int32), shifts.astype(jnp.int32))
    cuts = jax.random.randint(cut_key, (owners,), 0, 1 << 30) % (levels // 4 + 1)
    counts = jnp.maximum(levels - cuts, 1)
    fullest = jax.random.randint(full_key, (), 0, owners)
    counts = jnp.where(jnp.arange(owners) == fullest, C_SLOTS, counts)
    return counts.reshape(N_ROW, N_COL).astype(jnp.int32)


def level_of(stream_key, extent, cuts, least, high):
    level, own = 1.0, jax.random.fold_in(stream_key, 6)
    for axis_at, blocks in cuts:
        steps = jnp.exp(jax.random.uniform(jax.random.fold_in(own, axis_at), (blocks,), jnp.float32, least / len(cuts), high / len(cuts)))
        level = level * jnp.repeat(steps, extent[axis_at] // blocks).reshape([-1 if axis == axis_at else 1 for axis in range(len(extent))])
    return level


def noise(rng, dims, deviation, most, cuts=(), kind=jnp.bfloat16):
    values = jax.random.normal(rng, dims, jnp.float32) * deviation
    if len(cuts) > 0:
        values = level_of(rng, dims, cuts, -0.22, 0.18) * values
    return jnp.clip(values, min=-most, max=most).astype(kind)


def setup_inputs(seed: int = 0) -> dict:
    arg_keys = jax.random.split(jax.random.key(seed), 5)
    x_tiles = noise(arg_keys[0], (SECTIONS, SLAB_ROWS, SECTION_NNZ, TILE_EDGE, TILE_EDGE), 0.17, 1.0, ((0, 4), (1, 64)))
    x_cols = draw_x_cols(jax.random.fold_in(arg_keys[4], 71), 0)
    c_list = draw_c_list(jax.random.fold_in(arg_keys[4], 71), 0)
    c_count = draw_c_count(jax.random.fold_in(arg_keys[4], 71), 0)
    return {"x_tiles": x_tiles, "x_cols": x_cols, "c_list": c_list, "c_count": c_count}


def owner_block(a_tiles, a_cols, b_tiles, b_cols, slot_pairs, live_count):
    per_round = math.gcd(32, C_SLOTS)

    def one_round(first_slot):
        chosen_rows = lax.dynamic_slice_in_dim(slot_pairs, first_slot, per_round, 0)
        left_tiles = a_tiles[:, chosen_rows[:, 0]].astype(jnp.float32)
        right_tiles = b_tiles[:, chosen_rows[:, 1]].astype(jnp.float32)
        matches = a_cols[:, chosen_rows[:, 0]][:, :, :, None] == b_cols[:, chosen_rows[:, 1]][:, :, None, :]
        picked = jnp.sum(jnp.where(matches[..., None, None], right_tiles[:, :, None], jnp.float32(0.0)), axis=3)
        sectioned = jnp.einsum("sgpik,sgpjk->sgij", left_tiles, picked)
        layered = sectioned.reshape(N_LAYER, LOCAL_SECTIONS, per_round, TILE_EDGE, TILE_EDGE).sum(axis=1)
        rounded = lax.optimization_barrier(layered.astype(jnp.bfloat16)).astype(jnp.float32)
        summed = rounded.sum(axis=0)
        live_mask = (first_slot + jnp.arange(per_round, dtype=jnp.int32)) < live_count
        return jnp.where(live_mask[:, None, None], summed, jnp.float32(0.0))

    firsts = jnp.arange(C_SLOTS // per_round, dtype=jnp.int32) * per_round
    return lax.map(one_round, firsts).reshape(C_SLOTS, TILE_EDGE, TILE_EDGE)


def reference(x_tiles, x_cols, c_list, c_count):
    layout = x_tiles.reshape(SECTIONS, N_ROW, N_COL, ROWS_DEV, SECTION_NNZ, TILE_EDGE, TILE_EDGE)
    col_layout = x_cols.reshape(SECTIONS, N_ROW, N_COL, ROWS_DEV, SECTION_NNZ)

    def one_owner(owner_index):
        grid_row = owner_index // N_COL
        grid_col = owner_index % N_COL
        a_tiles = layout[:, grid_row].reshape(SECTIONS, A_ROWS, SECTION_NNZ, TILE_EDGE, TILE_EDGE)
        a_cols = col_layout[:, grid_row].reshape(SECTIONS, A_ROWS, SECTION_NNZ)
        b_tiles = layout[:, :, grid_col].reshape(SECTIONS, B_ROWS, SECTION_NNZ, TILE_EDGE, TILE_EDGE)
        b_cols = col_layout[:, :, grid_col].reshape(SECTIONS, B_ROWS, SECTION_NNZ)
        return owner_block(a_tiles, a_cols, b_tiles, b_cols, c_list[grid_row, grid_col], c_count[grid_row, grid_col])

    blocks = lax.map(one_owner, jnp.arange(N_ROW * N_COL, dtype=jnp.int32))
    return blocks.reshape(N_ROW, N_COL, C_SLOTS, TILE_EDGE, TILE_EDGE)
```

```python
import jax
import jax.numpy as jnp
from jax import lax
from jax.experimental import pallas as pl
from jax.experimental.pallas import tpu as pltpu
from jax.sharding import PartitionSpec as P

EDGE = 128
CHUNK = 8
ZERO = 64
MESH = pl.DeviceIdType.MESH


def kernel(
    x_ref, xc_ref, cl_ref, cnt_ref, out_ref,
    a, b, fs, fr, ns, nr, own, ca, cb, crow, csm, idx,
    loc, gsend, a_recv, b_recv, csend, ca_recv, cb_recv, cl_sem,
    f_send, f_recv, n_send, n_recv, o_sem,
):
    row, col, lay = lax.axis_index("row"), lax.axis_index("col"), lax.axis_index("layer")
    zl, y, core = col // 8, (col // 2) % 4, col % 2
    pcol = (col + 8) % 16
    dz = 2 * zl - 1

    def col_of(z, yy):
        return (z * 4 + yy) * 2 + core

    rp, rm, rf = (row + 1) % 4, (row + 3) % 4, (row + 2) % 4
    rd = (row + 4 + dz) % 4
    re = (row + 4 - dz) % 4
    yp, ym, yf = (y + 1) % 4, (y + 3) % 4, (y + 2) % 4
    lp, lm, lf = (lay + 1) % 4, (lay + 3) % 4, (lay + 2) % 4
    sib = col + 1 - 2 * core
    zp = 1 - zl

    here = pl.ds(0, 8)
    my = [pltpu.make_async_copy(x_ref, a.at[pl.ds(col * 16, 16)], loc.at[0]),
          pltpu.make_async_copy(x_ref, b.at[pl.ds(row * 16, 16)], loc.at[1])]
    for m in my:
        m.start()

    barrier = pltpu.get_barrier_semaphore()
    peers = []
    for k in range(1, 8):
        peers.append((row, ((col // 2 + k) % 8) * 2 + core, lay))
    for r in (rp, rm, rf):
        peers.append((r, col, lay))
    peers += [(row, sib, lay), (rd, pcol, lay), (row, col, lp), (row, col, lm)]
    for p in peers:
        pl.semaphore_signal(barrier, inc=1, device_id=p, device_id_type=MESH)

    lane = lax.broadcasted_iota(jnp.int32, (8, EDGE), 1)
    vals = jnp.zeros((8, EDGE), jnp.int32)
    for s in range(2):
        for k in range(4):
            for p in range(2):
                vals = jnp.where(lane == s * 8 + k * 2 + p, xc_ref[s, p, k], vals)
    cidx = zl * 4 + y
    ca[core, cidx] = vals
    cb[row] = vals
    b[ZERO] = jnp.zeros((EDGE, EDGE), jnp.bfloat16)

    pl.semaphore_wait(barrier, len(peers))

    started = []

    def send(src, dst, ssem, rsem, dev):
        d = pltpu.make_async_remote_copy(
            src_ref=src, dst_ref=dst, send_sem=ssem, recv_sem=rsem,
            device_id=dev, device_id_type=MESH)
        d.start()
        started.append(d)

    n = 0
    for k in range(1, 8):
        send(ca.at[core, cidx], ca.at[core, cidx], csend.at[n], ca_recv.at[cidx],
             (row, ((col // 2 + k) % 8) * 2 + core, lay))
        n += 1
    for r in (rp, rm, rf):
        send(cb.at[row], cb.at[row], csend.at[n], cb_recv.at[row], (r, col, lay))
        n += 1

    count = [0]

    def send_a(c, s, dev):
        part = a.at[pl.ds(c * 16 + s * 8, 8)]
        send(part, part, gsend.at[count[0]], a_recv.at[c, s], dev)
        count[0] += 1

    def send_b(r, s, dev):
        part = b.at[pl.ds(r * 16 + s * 8, 8)]
        send(part, part, gsend.at[count[0]], b_recv.at[r, s], dev)
        count[0] += 1

    def wait_a(c, s):
        part = a.at[pl.ds(c * 16 + s * 8, 8)]
        pltpu.make_async_remote_copy(
            src_ref=part, dst_ref=part, send_sem=gsend.at[0], recv_sem=a_recv.at[c, s],
            device_id=(row, sib, lay), device_id_type=MESH).wait_recv()

    def wait_b(r, s):
        part = b.at[pl.ds(r * 16 + s * 8, 8)]
        pltpu.make_async_remote_copy(
            src_ref=part, dst_ref=part, send_sem=gsend.at[0], recv_sem=b_recv.at[r, s],
            device_id=(row, sib, lay), device_id_type=MESH).wait_recv()

    to_p = (row, pcol, lay)
    to_yp, to_ym = (row, col_of(zl, yp), lay), (row, col_of(zl, ym), lay)
    to_sib = (row, sib, lay)
    to_d, to_pd = (rd, col, lay), (rd, pcol, lay)
    to_rp, to_rm = (rp, col, lay), (rm, col, lay)

    for m in my:
        m.wait()

    send_a(col, zl, to_p)
    send_a(col, 0, to_yp)
    send_a(col, 1, to_ym)
    send_a(col, zp, to_p)
    send_a(col, 1, to_yp)
    send_a(col, 0, to_ym)
    send_b(row, zp, to_d)
    send_b(row, zl, to_d)
    send_a(col, 0, to_sib)
    send_a(col, 1, to_sib)

    def pass_p(s):
        wait_a(pcol, s)
        send_a(pcol, s, to_yp)
        send_a(pcol, s, to_ym)
        part = a.at[pl.ds(pcol * 16 + s * 8, 8)]
        send(part, b.at[pl.ds(row * 16 + s * 8, 8)], gsend.at[count[0]],
             b_recv.at[row, s], to_pd)
        count[0] += 1
        send_a(pcol, s, to_sib)

    def pass_y(z):
        cm, cp = col_of(z, ym), col_of(z, yp)
        wait_a(cm, 0)
        send_a(cm, 0, to_yp)
        wait_a(cp, 1)
        send_a(cp, 1, to_ym)
        send_a(cm, 0, to_sib)
        send_a(cp, 1, to_sib)

    def rest_y(z):
        cm, cp = col_of(z, ym), col_of(z, yp)
        wait_a(cm, 1)
        send_a(cm, 1, to_sib)
        wait_a(cp, 0)
        send_a(cp, 0, to_sib)

    def far_y(z):
        cf = col_of(z, yf)
        for s in range(2):
            wait_a(cf, s)
            send_a(cf, s, to_sib)

    pass_p(zp)
    pass_y(zl)
    wait_b(re, zp)
    send_b(re, zp, to_d)
    pass_p(zl)
    rest_y(zl)
    wait_b(rd, zl)
    send_b(rd, zl, (re, col, lay))
    pass_y(zp)

    for k in range(1, 8):
        ci = (cidx + k) % 8
        pltpu.make_async_remote_copy(
            src_ref=ca.at[core, ci], dst_ref=ca.at[core, ci], send_sem=csend.at[0],
            recv_sem=ca_recv.at[ci], device_id=to_sib, device_id_type=MESH).wait_recv()
    send(ca.at[core], ca.at[core], csend.at[n], ca_recv.at[8], to_sib)
    for r in (rp, rm, rf):
        pltpu.make_async_remote_copy(
            src_ref=cb.at[r], dst_ref=cb.at[r], send_sem=csend.at[0],
            recv_sem=cb_recv.at[r], device_id=to_sib, device_id_type=MESH).wait_recv()
    pltpu.make_async_remote_copy(
        src_ref=ca.at[1 - core], dst_ref=ca.at[1 - core], send_sem=csend.at[0],
        recv_sem=ca_recv.at[8], device_id=to_sib, device_id_type=MESH).wait_recv()
    for c in range(16):
        crow[c : c + 1, :] = ca[c % 2, c // 2, 0:1, :]
    for r in range(4):
        crow[16 + r : 17 + r, :] = cb[r, 0:1, :]
    for r in range(4):
        crow[20 + r : 21 + r, :] = jnp.zeros((1, EDGE), jnp.int32)
    to_smem = pltpu.make_async_copy(crow, csm, cl_sem)
    to_smem.start()
    to_smem.wait()
    live = cnt_ref[0, 0]

    def prepare(t, carry):
        av, bv = cl_ref[0, t], cl_ref[1, t]
        ah, al = av >> 2, (av & 3) * 2
        bh, bl = bv >> 2, (bv & 3) * 2
        idx[0, t] = ah * 16 + al
        alive = t < live
        for s in range(2):
            base = bh * 16 + s * 8 + bl
            q0, q1 = csm[16 + bh, s * 8 + bl], csm[16 + bh, s * 8 + bl + 1]
            for p in range(2):
                have = csm[ah, s * 8 + al + p]
                at = jnp.where(have == q0, base, jnp.where(have == q1, base + 1, ZERO))
                idx[1 + s * 2 + p, t] = jnp.where(alive, at, ZERO)
        return carry

    lax.fori_loop(0, 256, prepare, 0)

    rest_y(zp)
    far_y(zl)
    far_y(zp)
    for z in range(2):
        for yy in range(4):
            c = (z * 4 + yy) * 2 + 1 - core
            wait_a(c, 0)
            wait_a(c, 1)
    wait_b(re, zl)
    wait_b(rd, zp)
    wait_b(rf, 0)
    wait_b(rf, 1)

    def product(t):
        ai = idx[0, t]
        left = jnp.concatenate([a[ai], a[ai + 1], a[ai + 8], a[ai + 9]], axis=1)
        right = jnp.concatenate([b[idx[1 + q, t]] for q in range(4)], axis=1)
        return lax.dot_general(left, right, (((1,), (1,)), ((), ())),
                               preferred_element_type=jnp.float32)

    def rs_copy(src, dst, ssem, rsem, dev):
        return pltpu.make_async_remote_copy(
            src_ref=src, dst_ref=dst, send_sem=ssem, recv_sem=rsem,
            device_id=dev, device_id_type=MESH)

    ring = [(row, col, lp), (row, col, lm)]
    UNROLL = 4

    def slots(body):
        def step(i, carry):
            for u in range(UNROLL):
                body(i * UNROLL + u)
            return carry
        lax.fori_loop(0, CHUNK // UNROLL, step, 0)

    def f_copy(d, k):
        part = pl.ds(k * CHUNK, CHUNK)
        return rs_copy(fs.at[d, part], fr.at[d, part], f_send.at[d, k], f_recv.at[d, k], ring[d])

    def n_copy(d, k):
        part = pl.ds(k * CHUNK, CHUNK)
        return rs_copy(ns.at[d, part], nr.at[d, part], n_send.at[d, k], n_recv.at[d, k], ring[d])

    KH = 32 // CHUNK

    def far(k, carry):
        for d in range(2):
            base = lf * 64 + d * 32 + k * CHUNK
            slots(lambda i: fs.__setitem__((d, k * CHUNK + i), product(base + i).astype(jnp.bfloat16)))
            f_copy(d, k).start()
        return carry

    lax.fori_loop(0, KH, far, 0)

    def near(k, carry):
        for d, owner in ((0, lp), (1, lm)):
            at = (1 - d) * 32 + k * CHUNK
            base = owner * 64 + at
            slots(lambda i: ns.__setitem__((d, at + i), product(base + i).astype(jnp.bfloat16)))
            n_copy(d, (1 - d) * KH + k).start()
        return carry

    lax.fori_loop(0, KH, near, 0)

    def both(k, carry):
        for d, owner in ((0, lp), (1, lm)):
            at = d * 32 + k * CHUNK
            base = owner * 64 + at
            f_copy(d, k).wait_recv()
            slots(lambda i: ns.__setitem__(
                (d, at + i),
                (product(base + i) + fr[d, k * CHUNK + i].astype(jnp.float32)).astype(jnp.bfloat16)))
            n_copy(d, d * KH + k).start()
        return carry

    lax.fori_loop(0, KH, both, 0)

    def mine(k, carry):
        base = lay * 64 + k * CHUNK
        slots(lambda i: own.__setitem__(k * CHUNK + i, product(base + i)))
        return carry

    lax.fori_loop(0, 2 * KH, mine, 0)

    def o_copy(k):
        part = pl.ds(k * CHUNK, CHUNK)
        return pltpu.make_async_copy(own.at[part], out_ref.at[part], o_sem.at[k])

    def finish(k, carry):
        for d in range(2):
            at = d * KH + k
            n_copy(1 - d, at).wait_recv()
            n_copy(d, at).wait_recv()
            part = pl.ds(at * CHUNK, CHUNK)
            own[part] = own[part] + (nr[0, part].astype(jnp.float32) + nr[1, part].astype(jnp.float32))
            o_copy(at).start()
        return carry

    lax.fori_loop(0, KH, finish, 0)

    for d in started:
        d.wait_send()
    for d in range(2):
        lax.fori_loop(0, KH, lambda k, c: (f_copy(d, k).wait_send(), c)[1], 0)
        lax.fori_loop(0, 2 * KH, lambda k, c: (n_copy(d, k).wait_send(), c)[1], 0)
    lax.fori_loop(0, 2 * KH, lambda k, c: (o_copy(k).wait(), c)[1], 0)


def on_device(x_tiles, x_cols, c_list, c_count):
    hbm, smem = pl.BlockSpec(memory_space=pl.ANY), pl.BlockSpec(memory_space=pltpu.SMEM)
    tile = (EDGE, EDGE)
    dma = pltpu.SemaphoreType.DMA
    out = pl.pallas_call(
        kernel,
        out_shape=jax.ShapeDtypeStruct((64,) + tile, jnp.float32),
        in_specs=[hbm, smem, smem, smem],
        out_specs=hbm,
        scratch_shapes=[
            pltpu.VMEM((256,) + tile, jnp.bfloat16),
            pltpu.VMEM((65,) + tile, jnp.bfloat16),
            pltpu.VMEM((2, 32) + tile, jnp.bfloat16),
            pltpu.VMEM((2, 32) + tile, jnp.bfloat16),
            pltpu.VMEM((2, 64) + tile, jnp.bfloat16),
            pltpu.VMEM((2, 64) + tile, jnp.bfloat16),
            pltpu.VMEM((64,) + tile, jnp.float32),
            pltpu.VMEM((2, 8, 8, EDGE), jnp.int32),
            pltpu.VMEM((4, 8, EDGE), jnp.int32),
            pltpu.VMEM((24, EDGE), jnp.int32),
            pltpu.SMEM((24, EDGE), jnp.int32),
            pltpu.SMEM((8, 256), jnp.int32),
            dma((2,)), dma((48,)), dma((16, 2)), dma((4, 2)),
            dma((11,)), dma((9,)), dma((4,)), dma,
            dma((2, 32 // CHUNK)), dma((2, 32 // CHUNK)),
            dma((2, 64 // CHUNK)), dma((2, 64 // CHUNK)), dma((64 // CHUNK,)),
        ],
        compiler_params=pltpu.CompilerParams(
            collective_id=0, has_side_effects=True, vmem_limit_bytes=52 * 1024 * 1024),
    )(x_tiles.reshape((16,) + tile), jnp.swapaxes(x_cols, 1, 2),
      jnp.swapaxes(c_list[0, 0], 0, 1), c_count)
    return out[None, None]


def solution(mesh):
    return jax.shard_map(
        on_device,
        mesh=mesh,
        in_specs=(
            P("layer", ("row", "col"), None, None, None),
            P("layer", ("row", "col"), None),
            P("row", "col", None, None),
            P("row", "col"),
        ),
        out_specs=P("row", "col", "layer", None, None),
        check_vma=False,
    )
```

```python
import jax
import jax.numpy as jnp
from jax import lax
from jax.experimental import pallas as pl
from jax.experimental.pallas import tpu as pltpu
from jax.sharding import PartitionSpec as P

EDGE = 128
HALF = 64
A_HALF = 256
B_HALF = 65
ZERO = 64
PAIRS = 16
Q_CHUNK = 8
R_CHUNK = 4
Q_PARTS = PAIRS // Q_CHUNK
R_PARTS = PAIRS // R_CHUNK
MESH = pl.DeviceIdType.MESH


def kernel(
    x_hbm, cols_hbm, list_hbm, count, out_ref,
    a0, a1, b0, b1, fq_out, fq_in, fr_out, fr_in, nq_out, nq_in, nr_out, nr_in,
    ca, cb, cols, pairs, idv, idx,
    loc, small, gsend, a_recv, b_recv, csend, ca_recv, cb_recv,
    fq_send, fq_recv, fr_send, fr_recv, nq_send, nq_recv, nr_send, nr_recv,
):
    row, col, lay = lax.axis_index("row"), lax.axis_index("col"), lax.axis_index("layer")
    zl, y, core = col // 8, (col // 2) % 4, col % 2
    zp = 1 - zl
    a, b = (a0, a1), (b0, b1)
    pcol = (col + 8) % 16
    sib = col + 1 - 2 * core
    dz = 2 * zl - 1
    cidx = zl * 4 + y

    def col_of(z, yy):
        return (z * 4 + yy) * 2 + core

    rp, rm, rf = (row + 1) % 4, (row + 3) % 4, (row + 2) % 4
    rd, re = (row + 4 + dz) % 4, (row + 4 - dz) % 4
    yp, ym, yf = (y + 1) % 4, (y + 3) % 4, (y + 2) % 4
    lp, lm, lf = (lay + 1) % 4, (lay + 3) % 4, (lay + 2) % 4

    def a_part(c, h, s):
        return a[h].at[pl.ds(c * 16 + s * 8, 8)]

    def b_part(r, h, s):
        return b[h].at[pl.ds(r * 16 + s * 8, 8)]

    cols_in = pltpu.make_async_copy(cols_hbm, cols, small.at[0])
    list_in = pltpu.make_async_copy(list_hbm, pairs, small.at[1])
    own_in = []
    for h in range(2):
        rows = x_hbm.at[:, pl.ds(h * HALF, HALF)]
        own_in.append((
            pltpu.make_async_copy(rows, a[h].at[pl.ds(col * 16, 16)], loc.at[h, 0]),
            pltpu.make_async_copy(rows, b[h].at[pl.ds(row * 16, 16)], loc.at[h, 1])))
    cols_in.start()
    for pair in own_in:
        for m in pair:
            m.start()
    list_in.start()

    barrier = pltpu.get_barrier_semaphore()
    chips = [(row, ((col // 2 + k) % 8) * 2 + core, lay) for k in range(1, 8)]
    ends = [(r, col, lay) for r in (rp, rm, rf)]
    peers = chips + ends + [(row, sib, lay), (rd, pcol, lay), (row, col, lp), (row, col, lm)]
    for p in peers:
        pl.semaphore_signal(barrier, inc=1, device_id=p, device_id_type=MESH)

    cols_in.wait()
    lane = lax.broadcasted_iota(jnp.int32, (8, EDGE), 1)
    sub = lax.broadcasted_iota(jnp.int32, (8, EDGE), 0)
    for first, where in ((col * 4, ca.at[core, cidx]), (row * 4, cb.at[row])):
        vals = jnp.zeros((8, EDGE), jnp.int32)
        for s in range(2):
            for k in range(4):
                for p in range(2):
                    vals = jnp.where((lane == first + k) & (sub == s * 2 + p), cols[s, p, k], vals)
        where[...] = vals
    for h in range(2):
        b[h][ZERO] = jnp.zeros((HALF, EDGE), jnp.bfloat16)

    pl.semaphore_wait(barrier, len(peers))

    started = []

    def copy_to(src, dst, ssem, rsem, dev):
        return pltpu.make_async_remote_copy(
            src_ref=src, dst_ref=dst, send_sem=ssem, recv_sem=rsem,
            device_id=dev, device_id_type=MESH)

    def send(src, dst, ssem, rsem, dev):
        d = copy_to(src, dst, ssem, rsem, dev)
        d.start()
        started.append(d)

    to_sib = (row, sib, lay)
    to_p, to_d, to_pd, to_e = (row, pcol, lay), (rd, col, lay), (rd, pcol, lay), (re, col, lay)
    to_yp, to_ym = (row, col_of(zl, yp), lay), (row, col_of(zl, ym), lay)

    for n, dev in enumerate(chips):
        send(ca.at[core, cidx], ca.at[core, cidx], csend.at[n], ca_recv.at[cidx], dev)
    for n, dev in enumerate(ends):
        send(cb.at[row], cb.at[row], csend.at[7 + n], cb_recv.at[row], dev)

    used = [0]

    def next_sem():
        used[0] += 1
        return gsend.at[used[0] - 1]

    def send_a(c, h, s, dev):
        send(a_part(c, h, s), a_part(c, h, s), next_sem(), a_recv.at[h, c, s], dev)

    def send_b(r, h, s, dev):
        send(b_part(r, h, s), b_part(r, h, s), next_sem(), b_recv.at[h, r, s], dev)

    def wait_a(c, h, s):
        copy_to(a_part(c, h, s), a_part(c, h, s), gsend.at[0], a_recv.at[h, c, s], to_sib).wait_recv()

    def wait_b(r, h, s):
        copy_to(b_part(r, h, s), b_part(r, h, s), gsend.at[0], b_recv.at[h, r, s], to_sib).wait_recv()

    def own_block(h):
        for m in own_in[h]:
            m.wait()
        send_a(col, h, zl, to_p)
        send_a(col, h, 0, to_yp)
        send_a(col, h, 1, to_ym)
        send_b(row, h, zp, to_d)
        send_a(col, h, zp, to_p)
        send_a(col, h, 1, to_yp)
        send_a(col, h, 0, to_ym)
        send_b(row, h, zl, to_d)
        send_a(col, h, 0, to_sib)
        send_a(col, h, 1, to_sib)

    def pass_p(h, s):
        wait_a(pcol, h, s)
        send_a(pcol, h, s, to_yp)
        send_a(pcol, h, s, to_ym)
        send(a_part(pcol, h, s), b_part(row, h, s), next_sem(), b_recv.at[h, row, s], to_pd)
        send_a(pcol, h, s, to_sib)

    def pass_y(h, z):
        cm, cp = col_of(z, ym), col_of(z, yp)
        wait_a(cm, h, 0)
        send_a(cm, h, 0, to_yp)
        wait_a(cp, h, 1)
        send_a(cp, h, 1, to_ym)
        send_a(cm, h, 0, to_sib)
        send_a(cp, h, 1, to_sib)

    def rest_y(h, z):
        cm, cp = col_of(z, ym), col_of(z, yp)
        wait_a(cm, h, 1)
        send_a(cm, h, 1, to_sib)
        wait_a(cp, h, 0)
        send_a(cp, h, 0, to_sib)

    def far_y(h, z):
        cf = col_of(z, yf)
        for s in range(2):
            wait_a(cf, h, s)
            send_a(cf, h, s, to_sib)

    def far_b(h, which):
        if which == 0:
            wait_b(re, h, zp)
            send_b(re, h, zp, to_d)
        else:
            wait_b(rd, h, zl)
            send_b(rd, h, zl, to_e)

    def last(h):
        for z in range(2):
            for yy in range(4):
                c = (z * 4 + yy) * 2 + 1 - core
                wait_a(c, h, 0)
                wait_a(c, h, 1)
        wait_b(re, h, zl)
        wait_b(rd, h, zp)
        wait_b(rf, h, 0)
        wait_b(rf, h, 1)

    own_block(0)
    pass_y(0, zl)
    pass_p(0, zp)
    far_b(0, 0)
    pass_p(0, zl)
    rest_y(0, zl)
    pass_y(0, zp)
    far_b(0, 1)
    own_block(1)

    for k in range(1, 8):
        ci = (cidx + k) % 8
        copy_to(ca.at[core, ci], ca.at[core, ci], csend.at[0], ca_recv.at[ci], to_sib).wait_recv()
    send(ca.at[core], ca.at[core], csend.at[10], ca_recv.at[8], to_sib)
    for r in (rp, rm, rf):
        copy_to(cb.at[r], cb.at[r], csend.at[0], cb_recv.at[r], to_sib).wait_recv()
    copy_to(ca.at[1 - core], ca.at[1 - core], csend.at[0], ca_recv.at[8], to_sib).wait_recv()
    list_in.wait()
    acols = jnp.sum(ca[...].reshape(16, 8, EDGE), axis=0)
    bcols = jnp.sum(cb[...], axis=0)
    live = count[0, 0]
    for g in range(2):
        part = slice(g * EDGE, (g + 1) * EDGE)
        av = jnp.broadcast_to(pairs[0:1, part], (8, EDGE))
        bv = jnp.broadcast_to(pairs[1:2, part], (8, EDGE))
        have = jnp.take_along_axis(acols, av, axis=1, mode="promise_in_bounds")
        want = jnp.take_along_axis(bcols, bv, axis=1, mode="promise_in_bounds")
        ra, rb = av[0:1], bv[0:1]
        idv[0:1, part] = (ra >> 2) * 16 + (ra & 3) * 2
        alive = (lane[0:1] + g * EDGE) < live
        for s in range(2):
            base = (rb >> 2) * 16 + s * 8 + (rb & 3) * 2
            w0, w1 = want[s * 2 : s * 2 + 1], want[s * 2 + 1 : s * 2 + 2]
            for p in range(2):
                q = s * 2 + p
                h0 = have[q : q + 1]
                at = jnp.where(h0 == w0, base, jnp.where(h0 == w1, base + 1, ZERO))
                idv[1 + q : 2 + q, part] = jnp.where(alive, at, ZERO)
    idv[5:8, :] = jnp.zeros((3, 256), jnp.int32)
    to_smem = pltpu.make_async_copy(idv, idx, small.at[2])
    to_smem.start()
    to_smem.wait()

    rest_y(0, zp)
    far_y(0, zl)
    far_y(0, zp)
    last(0)

    def left_of(t, h):
        u = idx[0, t]
        return jnp.concatenate([a[h][u], a[h][u + 1], a[h][u + 8], a[h][u + 9]], axis=1)

    def right_of(t, h):
        return jnp.concatenate([b[h][idx[1 + q, t]] for q in range(4)], axis=1)

    def times(left, right):
        return lax.dot_general(left, right, (((1,), (1,)), ((), ())),
                               preferred_element_type=jnp.float32)

    low = lax.broadcasted_iota(jnp.int32, (HALF, EDGE), 1) < HALF

    def quadrants(t):
        both = times(jnp.concatenate([left_of(t, 0), left_of(t + 1, 0)], axis=0),
                     jnp.concatenate([right_of(t, 0), right_of(t + 1, 0)], axis=0))
        return jnp.where(low, both[:HALF], both[HALF:])

    def whole(t):
        return times(jnp.concatenate([left_of(t, 0), left_of(t, 1)], axis=0),
                     jnp.concatenate([right_of(t, 0), right_of(t, 1)], axis=0))

    def rest(t):
        one, two = whole(t), whole(t + 1)
        mixed = jnp.where(low, pltpu.roll(two[:HALF], HALF, 1), one[:HALF])
        return mixed, one[HALF:], two[HALF:]

    ring = [(row, col, lp), (row, col, lm)]

    def fq(d, k):
        part = pl.ds(k * Q_CHUNK, Q_CHUNK)
        return copy_to(fq_out.at[d, part], fq_in.at[d, part], fq_send.at[d, k], fq_recv.at[d, k], ring[d])

    def fr(d, k):
        part = pl.ds(k * R_CHUNK, R_CHUNK)
        return copy_to(fr_out.at[d, part], fr_in.at[d, part], fr_send.at[d, k], fr_recv.at[d, k], ring[d])

    def nq(d, g, k):
        part = pl.ds(k * Q_CHUNK, Q_CHUNK)
        return copy_to(nq_out.at[d, g, part], nq_in.at[d, g, part], nq_send.at[d, g, k],
                       nq_recv.at[d, g, k], ring[d])

    def nr(d, g, k):
        part = pl.ds(k * R_CHUNK, R_CHUNK)
        return copy_to(nr_out.at[d, g, part], nr_in.at[d, g, part], nr_send.at[d, g, k],
                       nr_recv.at[d, g, k], ring[d])

    def each(n, body, unroll):
        def step(i, carry):
            for u in range(unroll):
                body(i * unroll + u)
            return carry
        lax.fori_loop(0, n // unroll, step, 0)

    def half(v):
        return v.astype(jnp.bfloat16)

    def wide(v):
        return v.astype(jnp.float32)

    next_owner = (lp, lm)

    def far_q(k):
        for d in range(2):
            def body(i):
                j = k * Q_CHUNK + i
                fq_out[d, j] = half(quadrants(lf * 64 + d * 32 + 2 * j))
            each(Q_CHUNK, body, 4)
            fq(d, k).start()

    def near_q(k):
        for d in range(2):
            g = 1 - d
            def body(i):
                j = k * Q_CHUNK + i
                nq_out[d, g, j] = half(quadrants(next_owner[d] * 64 + g * 32 + 2 * j))
            each(Q_CHUNK, body, 4)
            nq(d, g, k).start()

    def sum_q(k):
        for d in range(2):
            fq(d, k).wait_recv()
            def body(i):
                j = k * Q_CHUNK + i
                nq_out[d, d, j] = half(
                    quadrants(next_owner[d] * 64 + d * 32 + 2 * j) + wide(fq_in[d, j]))
            each(Q_CHUNK, body, 4)
            nq(d, d, k).start()

    def loop(n, body):
        def step(k, carry):
            body(k)
            return carry
        lax.fori_loop(0, n, step, 0)

    loop(Q_PARTS, far_q)
    pass_y(1, zl)
    pass_p(1, zp)
    loop(Q_PARTS, near_q)
    far_b(1, 0)
    pass_p(1, zl)
    rest_y(1, zl)
    loop(Q_PARTS, sum_q)
    pass_y(1, zp)
    far_b(1, 1)
    rest_y(1, zp)
    far_y(1, zl)
    far_y(1, zp)
    last(1)

    def far_r(k):
        for d in range(2):
            def body(i):
                j = k * R_CHUNK + i
                for n, v in enumerate(rest(lf * 64 + d * 32 + 2 * j)):
                    fr_out[d, j, n] = half(v)
            each(R_CHUNK, body, 2)
            fr(d, k).start()

    def near_r(k):
        for d in range(2):
            g = 1 - d
            def body(i):
                j = k * R_CHUNK + i
                for n, v in enumerate(rest(next_owner[d] * 64 + g * 32 + 2 * j)):
                    nr_out[d, g, j, n] = half(v)
            each(R_CHUNK, body, 2)
            nr(d, g, k).start()

    def sum_r(k):
        for d in range(2):
            fr(d, k).wait_recv()
            def body(i):
                j = k * R_CHUNK + i
                for n, v in enumerate(rest(next_owner[d] * 64 + d * 32 + 2 * j)):
                    nr_out[d, d, j, n] = half(v + wide(fr_in[d, j, n]))
            each(R_CHUNK, body, 2)
            nr(d, d, k).start()

    loop(R_PARTS, far_r)
    loop(R_PARTS, near_r)

    def mine(t):
        out_ref[t] = whole(lay * 64 + t)

    each(64, mine, 4)
    loop(R_PARTS, sum_r)

    for d in range(2):
        for g in range(2):
            loop(Q_PARTS, lambda k: nq(d, g, k).wait_recv())

    def finish(k):
        for g in range(2):
            for d in range(2):
                nr(d, g, k).wait_recv()

            def body(i):
                j = k * R_CHUNK + i
                t = g * 32 + 2 * j
                first = wide(nq_in[0, g, j]) + wide(nq_in[1, g, j])
                mixed, one, two = (wide(nr_in[0, g, j, n]) + wide(nr_in[1, g, j, n]) for n in range(3))
                upper, lower = pl.ds(0, HALF), pl.ds(HALF, HALF)
                out_ref[t, upper] += jnp.where(low, first, mixed)
                out_ref[t, lower] += one
                out_ref[t + 1, upper] += pltpu.roll(jnp.where(low, mixed, first), HALF, 1)
                out_ref[t + 1, lower] += two

            each(R_CHUNK, body, 2)

    loop(R_PARTS, finish)

    for d in started:
        d.wait_send()
    for d in range(2):
        loop(Q_PARTS, lambda k: fq(d, k).wait_send())
        loop(R_PARTS, lambda k: fr(d, k).wait_send())
        for g in range(2):
            loop(Q_PARTS, lambda k: nq(d, g, k).wait_send())
            loop(R_PARTS, lambda k: nr(d, g, k).wait_send())


def on_device(x_tiles, x_cols, c_list, c_count):
    hbm = pl.BlockSpec(memory_space=pltpu.HBM)
    unit = (HALF, EDGE)
    dma = pltpu.SemaphoreType.DMA
    bf16 = lambda *dims: pltpu.VMEM(dims + unit, jnp.bfloat16)
    ints = lambda *dims: pltpu.VMEM(dims, jnp.int32)
    operands = [
        pltpu.with_memory_space_constraint(v, pltpu.HBM)
        for v in (x_tiles.reshape(16, EDGE, EDGE), jnp.swapaxes(x_cols, 1, 2),
                  jnp.swapaxes(c_list[0, 0], 0, 1))
    ]
    out = pl.pallas_call(
        kernel,
        out_shape=pltpu.VMEM((64, EDGE, EDGE), jnp.float32),
        in_specs=[hbm] * 3 + [pl.BlockSpec(memory_space=pltpu.SMEM)],
        out_specs=pl.BlockSpec(memory_space=pltpu.VMEM),
        scratch_shapes=[
            bf16(A_HALF), bf16(A_HALF), bf16(B_HALF), bf16(B_HALF),
            bf16(2, PAIRS), bf16(2, PAIRS), bf16(2, PAIRS, 3), bf16(2, PAIRS, 3),
            bf16(2, 2, PAIRS), bf16(2, 2, PAIRS), bf16(2, 2, PAIRS, 3), bf16(2, 2, PAIRS, 3),
            ints(2, 8, 8, EDGE), ints(4, 8, EDGE),
            pltpu.SMEM((2, 2, 4), jnp.int32), ints(2, 256),
            ints(8, 256), pltpu.SMEM((8, 256), jnp.int32),
            dma((2, 2)), dma((3,)), dma((72,)), dma((2, 16, 2)), dma((2, 4, 2)),
            dma((11,)), dma((9,)), dma((4,)),
            dma((2, Q_PARTS)), dma((2, Q_PARTS)), dma((2, R_PARTS)), dma((2, R_PARTS)),
            dma((2, 2, Q_PARTS)), dma((2, 2, Q_PARTS)), dma((2, 2, R_PARTS)), dma((2, 2, R_PARTS)),
        ],
        compiler_params=pltpu.CompilerParams(
            collective_id=0, has_side_effects=True, vmem_limit_bytes=40 * 1024 * 1024),
    )(*operands, c_count)
    return out[None, None]


def solution(mesh):
    return jax.shard_map(
        on_device,
        mesh=mesh,
        in_specs=(
            P("layer", ("row", "col"), None, None, None),
            P("layer", ("row", "col"), None),
            P("row", "col", None, None),
            P("row", "col"),
        ),
        out_specs=P("row", "col", "layer", None, None),
        check_vma=False,
    )
```

```python
import jax
import jax.numpy as jnp
from jax import lax
from jax.experimental import pallas as pl
from jax.experimental.pallas import tpu as pltpu
from jax.sharding import PartitionSpec as P

EDGE = 128
HALF = 64
ROWS = (64, 32, 32)
FIRST = (0, 64, 96)
A_UNITS = 256
B_UNITS = 65
ZERO = 64
PAIRS = 16
Q_PARTS, S_PARTS, R_PARTS = 4, 2, 4
MESH = pl.DeviceIdType.MESH
ORDER = (
    "0in", "0zp1", "0zp2", "0y0", "0y1", "0sb", "0d1", "0cols", "0q1", "0p1", "0d2", "0lists",
    "0p2", "0r1", "0b1", "0places", "0q2", "1in", "1y0", "1y1", "1zp1", "1zp2", "0b0", "1d1",
    "1d2", "1sb", "0r2", "0f1", "0f2", "0lastA", "0lastB", "0list", "F0", "F1", "1q1", "1p1",
    "F2", "F3", "1p2", "N0", "N1", "1r1", "2in", "2y0", "2y1", "2zp1", "2zp2", "2sb", "1b1",
    "1b0", "1q2", "N2", "N3", "2d1", "2d2", "S0", "S1", "2q1", "2p1", "S2", "S3", "1r2", "1f1",
    "1f2", "1lastA", "2p2", "f0", "f1", "2r1", "n0", "n1", "2b1", "2b0", "2q2", "s0", "s1",
    "2r2", "2f1", "2f2", "2lastA", "1lastB", "2lastB", "R",
)


def kernel(
    x_hbm, cols_hbm, list_hbm, count, out_ref,
    a0, a1, a2, b0, b1, b2, q_refs, s_refs, r_refs, ca, cb, cols, pairs, idv, idx,
    loc, small, gsend, a_recv, b_recv, csend, ca_recv, cb_recv,
    q_sems, s_sems, r_sems,
):
    row, col, lay = lax.axis_index("row"), lax.axis_index("col"), lax.axis_index("layer")
    zl, y, core = col // 8, (col // 2) % 4, col % 2
    zp = 1 - zl
    a, b = (a0, a1, a2), (b0, b1, b2)
    pcol = (col + 8) % 16
    sib = col + 1 - 2 * core
    dz = 2 * zl - 1
    cidx = zl * 4 + y

    def col_of(z, yy):
        return (z * 4 + yy) * 2 + core

    rp, rm, rf = (row + 1) % 4, (row + 3) % 4, (row + 2) % 4
    rd, re = (row + 4 + dz) % 4, (row + 4 - dz) % 4
    yp, ym, yf = (y + 1) % 4, (y + 3) % 4, (y + 2) % 4
    lp, lm, lf = (lay + 1) % 4, (lay + 3) % 4, (lay + 2) % 4

    def a_part(c, h, s):
        return a[h].at[pl.ds(c * 16 + s * 8, 8)]

    def b_part(r, h, s):
        return b[h].at[pl.ds(r * 16 + s * 8, 8)]

    cols_in = pltpu.make_async_copy(cols_hbm, cols, small.at[0])
    list_in = pltpu.make_async_copy(list_hbm, pairs, small.at[1])
    own_in = []
    for h in range(3):
        rows = x_hbm.at[:, pl.ds(FIRST[h], ROWS[h])]
        own_in.append((
            pltpu.make_async_copy(rows, a[h].at[pl.ds(col * 16, 16)], loc.at[h, 0]),
            pltpu.make_async_copy(rows, b[h].at[pl.ds(row * 16, 16)], loc.at[h, 1])))
    cols_in.start()
    for pair in own_in:
        for m in pair:
            m.start()
    list_in.start()

    barrier = pltpu.get_barrier_semaphore()
    chips = [(row, ((col // 2 + k) % 8) * 2 + core, lay) for k in range(1, 8)]
    ends = [(r, col, lay) for r in (rp, rm, rf)]
    peers = chips + ends + [(row, sib, lay), (rd, pcol, lay), (row, col, lp), (row, col, lm)]
    for p in peers:
        pl.semaphore_signal(barrier, inc=1, device_id=p, device_id_type=MESH)

    for h in range(3):
        b[h][ZERO] = jnp.zeros((ROWS[h], EDGE), jnp.bfloat16)

    pl.semaphore_wait(barrier, len(peers))

    started = []

    def copy_to(src, dst, ssem, rsem, dev):
        return pltpu.make_async_remote_copy(
            src_ref=src, dst_ref=dst, send_sem=ssem, recv_sem=rsem,
            device_id=dev, device_id_type=MESH)

    def send(src, dst, ssem, rsem, dev):
        d = copy_to(src, dst, ssem, rsem, dev)
        d.start()
        started.append(d)

    to_sib = (row, sib, lay)
    to_p, to_d, to_pd, to_e = (row, pcol, lay), (rd, col, lay), (rd, pcol, lay), (re, col, lay)
    to_yp, to_ym = (row, col_of(zl, yp), lay), (row, col_of(zl, ym), lay)

    used = [0]

    def next_sem():
        used[0] += 1
        return gsend.at[used[0] - 1]

    def send_a(c, h, s, dev):
        send(a_part(c, h, s), a_part(c, h, s), next_sem(), a_recv.at[h, c, s], dev)

    def send_b(r, h, s, dev):
        send(b_part(r, h, s), b_part(r, h, s), next_sem(), b_recv.at[h, r, s], dev)

    def wait_a(c, h, s):
        copy_to(a_part(c, h, s), a_part(c, h, s), gsend.at[0], a_recv.at[h, c, s], to_sib).wait_recv()

    def wait_b(r, h, s):
        copy_to(b_part(r, h, s), b_part(r, h, s), gsend.at[0], b_recv.at[h, r, s], to_sib).wait_recv()

    def own_to(h, step):
        if step == "zp1":
            send_a(col, h, zl, to_p)
        elif step == "zp2":
            send_a(col, h, zp, to_p)
        elif step == "y0":
            send_a(col, h, 0, to_yp)
            send_a(col, h, 1, to_ym)
        elif step == "y1":
            send_a(col, h, 1, to_yp)
            send_a(col, h, 0, to_ym)
        elif step == "d1":
            send_b(row, h, zp, to_d)
        elif step == "d2":
            send_b(row, h, zl, to_d)
        elif step == "sb":
            send_a(col, h, 0, to_sib)
            send_a(col, h, 1, to_sib)
        elif step == "list":
            to_smem.wait()
        elif step == "in":
            for m in own_in[h]:
                m.wait()

    def pass_p(h, s):
        wait_a(pcol, h, s)
        send_a(pcol, h, s, to_yp)
        send_a(pcol, h, s, to_ym)
        send(a_part(pcol, h, s), b_part(row, h, s), next_sem(), b_recv.at[h, row, s], to_pd)
        send_a(pcol, h, s, to_sib)

    def pass_y(h, z):
        cm, cp = col_of(z, ym), col_of(z, yp)
        wait_a(cm, h, 0)
        send_a(cm, h, 0, to_yp)
        wait_a(cp, h, 1)
        send_a(cp, h, 1, to_ym)
        send_a(cm, h, 0, to_sib)
        send_a(cp, h, 1, to_sib)

    def rest_y(h, z):
        cm, cp = col_of(z, ym), col_of(z, yp)
        wait_a(cm, h, 1)
        send_a(cm, h, 1, to_sib)
        wait_a(cp, h, 0)
        send_a(cp, h, 0, to_sib)

    def far_y(h, z):
        cf = col_of(z, yf)
        for s in range(2):
            wait_a(cf, h, s)
            send_a(cf, h, s, to_sib)

    def far_b(h, which):
        if which == 0:
            wait_b(re, h, zp)
            send_b(re, h, zp, to_d)
        else:
            wait_b(rd, h, zl)
            send_b(rd, h, zl, to_e)

    def last_a(h):
        for z in range(2):
            for yy in range(4):
                c = (z * 4 + yy) * 2 + 1 - core
                wait_a(c, h, 0)
                wait_a(c, h, 1)

    def last_b(h):
        wait_b(re, h, zl)
        wait_b(rd, h, zp)
        wait_b(rf, h, 0)
        wait_b(rf, h, 1)

    lane = lax.broadcasted_iota(jnp.int32, (8, EDGE), 1)

    def columns():
        cols_in.wait()
        sub = lax.broadcasted_iota(jnp.int32, (8, EDGE), 0)
        for first, where in ((col * 4, ca.at[core, cidx]), (row * 4, cb.at[row])):
            vals = jnp.zeros((8, EDGE), jnp.int32)
            for s in range(2):
                for k in range(4):
                    for p in range(2):
                        vals = jnp.where((lane == first + k) & (sub == s * 2 + p), cols[s, p, k], vals)
            where[...] = vals
        for n, dev in enumerate(chips):
            send(ca.at[core, cidx], ca.at[core, cidx], csend.at[n], ca_recv.at[cidx], dev)
        for n, dev in enumerate(ends):
            send(cb.at[row], cb.at[row], csend.at[7 + n], cb_recv.at[row], dev)

    to_smem = pltpu.make_async_copy(idv, idx, small.at[2])

    def lists():
        for k in range(1, 8):
            ci = (cidx + k) % 8
            copy_to(ca.at[core, ci], ca.at[core, ci], csend.at[0], ca_recv.at[ci], to_sib).wait_recv()
        send(ca.at[core], ca.at[core], csend.at[10], ca_recv.at[8], to_sib)

    def places():
        for r in (rp, rm, rf):
            copy_to(cb.at[r], cb.at[r], csend.at[0], cb_recv.at[r], to_sib).wait_recv()
        copy_to(ca.at[1 - core], ca.at[1 - core], csend.at[0], ca_recv.at[8], to_sib).wait_recv()
        list_in.wait()
        acols = jnp.sum(ca[...].reshape(16, 8, EDGE), axis=0)
        bcols = jnp.sum(cb[...], axis=0)
        live = count[0, 0]
        for g in range(2):
            part = slice(g * EDGE, (g + 1) * EDGE)
            av = jnp.broadcast_to(pairs[0:1, part], (8, EDGE))
            bv = jnp.broadcast_to(pairs[1:2, part], (8, EDGE))
            have = jnp.take_along_axis(acols, av, axis=1, mode="promise_in_bounds")
            want = jnp.take_along_axis(bcols, bv, axis=1, mode="promise_in_bounds")
            ra, rb = av[0:1], bv[0:1]
            idv[0:1, part] = (ra >> 2) * 16 + (ra & 3) * 2
            alive = (lane[0:1] + g * EDGE) < live
            for s in range(2):
                base = (rb >> 2) * 16 + s * 8 + (rb & 3) * 2
                w0, w1 = want[s * 2 : s * 2 + 1], want[s * 2 + 1 : s * 2 + 2]
                for p in range(2):
                    q = s * 2 + p
                    h0 = have[q : q + 1]
                    at = jnp.where(h0 == w0, base, jnp.where(h0 == w1, base + 1, ZERO))
                    idv[1 + q : 2 + q, part] = jnp.where(alive, at, ZERO)
        idv[5:8, :] = jnp.zeros((3, 256), jnp.int32)
        to_smem.start()

    steps = {
        "p1": lambda h: pass_p(h, zp), "p2": lambda h: pass_p(h, zl),
        "q1": lambda h: pass_y(h, zl), "q2": lambda h: pass_y(h, zp),
        "r1": lambda h: rest_y(h, zl), "r2": lambda h: rest_y(h, zp),
        "f1": lambda h: far_y(h, zl), "f2": lambda h: far_y(h, zp),
        "b0": lambda h: far_b(h, 0), "b1": lambda h: far_b(h, 1), "lastA": last_a, "lastB": last_b,
        "cols": lambda h: columns(), "lists": lambda h: lists(), "places": lambda h: places(),
    }

    def left_of(t, h):
        u = idx[0, t]
        return jnp.concatenate([a[h][u], a[h][u + 1], a[h][u + 8], a[h][u + 9]], axis=1)

    def right_of(t, h):
        return jnp.concatenate([b[h][idx[1 + q, t]] for q in range(4)], axis=1)

    def times(left, right):
        return lax.dot_general(left, right, (((1,), (1,)), ((), ())),
                               preferred_element_type=jnp.float32)

    low = lax.broadcasted_iota(jnp.int32, (96, EDGE), 1) < HALF

    def quadrants(t):
        both = times(jnp.concatenate([left_of(t, 0), left_of(t + 1, 0)], axis=0),
                     jnp.concatenate([right_of(t, 0), right_of(t + 1, 0)], axis=0))
        return jnp.where(low[:HALF], both[:HALF], both[HALF:])

    def strips(t):
        both = times(jnp.concatenate([left_of(t, 1), left_of(t + 1, 1)], axis=0),
                     jnp.concatenate([right_of(t, 0), right_of(t + 1, 0)], axis=0))
        return jnp.where(low[:32], both[:32], both[32:])

    def whole(t):
        return times(jnp.concatenate([left_of(t, h) for h in range(3)], axis=0),
                     jnp.concatenate([right_of(t, h) for h in range(3)], axis=0))

    def rest(t):
        one, two = whole(t), whole(t + 1)
        mixed = jnp.where(low, pltpu.roll(two[:96], HALF, 1), one[:96])
        return jnp.concatenate([mixed, one[96:], two[96:]], axis=0)

    def half(v):
        return v.astype(jnp.bfloat16)

    def wide(v):
        return v.astype(jnp.float32)

    def each(n, body, unroll):
        def step(i, carry):
            for u in range(unroll):
                body(i * unroll + u)
            return carry
        lax.fori_loop(0, n // unroll, step, 0)

    def loop(n, body):
        def step(k, carry):
            body(k)
            return carry
        lax.fori_loop(0, n, step, 0)

    ring = [(row, col, lp), (row, col, lm)]
    next_owner = (lp, lm)

    class Piece:
        def __init__(self, refs, sems, value, unroll):
            self.f_out, self.f_in, self.n_out, self.n_in = refs
            self.f_send, self.f_recv, self.n_send, self.n_recv = sems
            self.value, self.unroll = value, unroll
            self.parts = self.f_send.shape[1]
            self.chunk = PAIRS // self.parts

        def f_copy(self, d, k):
            part = pl.ds(k * self.chunk, self.chunk)
            return copy_to(self.f_out.at[d, part], self.f_in.at[d, part],
                           self.f_send.at[d, k], self.f_recv.at[d, k], ring[d])

        def n_copy(self, d, g, k):
            part = pl.ds(k * self.chunk, self.chunk)
            return copy_to(self.n_out.at[d, g, part], self.n_in.at[d, g, part],
                           self.n_send.at[d, g, k], self.n_recv.at[d, g, k], ring[d])

        def far(self, k):
            for d in range(2):
                def body(i):
                    j = k * self.chunk + i
                    self.f_out[d, j] = half(self.value(lf * 64 + d * 32 + 2 * j))
                each(self.chunk, body, self.unroll)
                self.f_copy(d, k).start()

        def near(self, k):
            for d in range(2):
                g = 1 - d
                def body(i):
                    j = k * self.chunk + i
                    self.n_out[d, g, j] = half(self.value(next_owner[d] * 64 + g * 32 + 2 * j))
                each(self.chunk, body, self.unroll)
                self.n_copy(d, g, k).start()

        def sum(self, k):
            for d in range(2):
                self.f_copy(d, k).wait_recv()
                def body(i):
                    j = k * self.chunk + i
                    own = self.value(next_owner[d] * 64 + d * 32 + 2 * j)
                    self.n_out[d, d, j] = half(own + wide(self.f_in[d, j]))
                each(self.chunk, body, self.unroll)
                self.n_copy(d, d, k).start()

        def arrived(self, g, k):
            for d in range(2):
                self.n_copy(d, g, k).wait_recv()

        def sent(self):
            for d in range(2):
                loop(self.parts, lambda k: self.f_copy(d, k).wait_send())
                for g in range(2):
                    loop(self.parts, lambda k: self.n_copy(d, g, k).wait_send())

        def total(self, g, j):
            return wide(self.n_in[0, g, j]) + wide(self.n_in[1, g, j])

    corner = Piece(q_refs, q_sems, quadrants, 4)
    strip = Piece(s_refs, s_sems, strips, 4)
    remainder = Piece(r_refs, r_sems, rest, 2)

    def mine(t):
        out_ref[t] = whole(lay * 64 + t)

    def remaining():
        loop(remainder.parts, remainder.far)
        loop(remainder.parts, remainder.near)
        each(64, mine, 4)
        loop(remainder.parts, remainder.sum)

    kinds = {"F": corner.far, "N": corner.near, "S": corner.sum,
             "f": strip.far, "n": strip.near, "s": strip.sum}
    for word in ORDER:
        if word == "R":
            remaining()
        elif word[0] in kinds:
            kinds[word[0]](int(word[1:] or 0))
        elif word[1:] in steps:
            steps[word[1:]](int(word[0]))
        else:
            own_to(int(word[0]), word[1:])

    for g in range(2):
        for piece in (corner, strip):
            loop(piece.parts, lambda k: piece.arrived(g, k))

    def finish(k):
        for g in range(2):
            remainder.arrived(g, k)

            def body(i):
                j = k * remainder.chunk + i
                t = g * 32 + 2 * j
                first = jnp.concatenate([corner.total(g, j), strip.total(g, j)], axis=0)
                more = remainder.total(g, j)
                mixed = more[:96]
                upper, lower = pl.ds(0, 96), pl.ds(96, 32)
                out_ref[t, upper] += jnp.where(low, first, mixed)
                out_ref[t, lower] += more[96:128]
                out_ref[t + 1, upper] += pltpu.roll(jnp.where(low, mixed, first), HALF, 1)
                out_ref[t + 1, lower] += more[128:]

            each(remainder.chunk, body, 2)

    loop(remainder.parts, finish)

    for d in started:
        d.wait_send()
    for piece in (corner, strip, remainder):
        piece.sent()


def on_device(x_tiles, x_cols, c_list, c_count):
    hbm = pl.BlockSpec(memory_space=pltpu.HBM)
    dma = pltpu.SemaphoreType.DMA
    bf16 = lambda *dims: pltpu.VMEM(dims + (EDGE,), jnp.bfloat16)
    ints = lambda *dims: pltpu.VMEM(dims, jnp.int32)
    buffers = lambda n: [bf16(2, PAIRS, n), bf16(2, PAIRS, n), bf16(2, 2, PAIRS, n), bf16(2, 2, PAIRS, n)]
    semaphores = lambda n: [dma((2, n)), dma((2, n)), dma((2, 2, n)), dma((2, 2, n))]
    operands = [
        pltpu.with_memory_space_constraint(v, pltpu.HBM)
        for v in (x_tiles.reshape(16, EDGE, EDGE), jnp.swapaxes(x_cols, 1, 2),
                  jnp.swapaxes(c_list[0, 0], 0, 1))
    ]
    out = pl.pallas_call(
        kernel,
        out_shape=pltpu.VMEM((64, EDGE, EDGE), jnp.float32),
        in_specs=[hbm] * 3 + [pl.BlockSpec(memory_space=pltpu.SMEM)],
        out_specs=pl.BlockSpec(memory_space=pltpu.VMEM),
        scratch_shapes=[
            *[bf16(A_UNITS, n) for n in ROWS], *[bf16(B_UNITS, n) for n in ROWS],
            buffers(64), buffers(32), buffers(160),
            ints(2, 8, 8, EDGE), ints(4, 8, EDGE),
            pltpu.SMEM((2, 2, 4), jnp.int32), ints(2, 256),
            ints(8, 256), pltpu.SMEM((8, 256), jnp.int32),
            dma((3, 2)), dma((3,)), dma((108,)), dma((3, 16, 2)), dma((3, 4, 2)),
            dma((11,)), dma((9,)), dma((4,)),
            semaphores(Q_PARTS), semaphores(S_PARTS), semaphores(R_PARTS),
        ],
        compiler_params=pltpu.CompilerParams(
            collective_id=0, has_side_effects=True, vmem_limit_bytes=40 * 1024 * 1024),
    )(*operands, c_count)
    return out[None, None]


def solution(mesh):
    return jax.shard_map(
        on_device,
        mesh=mesh,
        in_specs=(
            P("layer", ("row", "col"), None, None, None),
            P("layer", ("row", "col"), None),
            P("row", "col", None, None),
            P("row", "col"),
        ),
        out_specs=P("row", "col", "layer", None, None),
        check_vma=False,
    )
```

```python
import jax
import jax.numpy as jnp
from jax import lax
from jax.experimental import pallas as pl
from jax.experimental.pallas import tpu as pltpu
from jax.sharding import PartitionSpec as P

EDGE = 128
HALF = 64
ROWS = (64, 32, 32)
FIRST = (0, 64, 96)
A_UNITS = 256
B_UNITS = 65
ZERO = 64
PAIRS = 16
Q_PARTS, S_PARTS, R_PARTS = 2, 1, 4
MESH = pl.DeviceIdType.MESH
ORDER = (
    "0in", "0zp1", "0zp2", "0y0", "0y1", "0sb", "0d1", "0cols", "0q1", "0p1", "0d2", "0lists",
    "0p2", "0r1", "0b1", "0places", "0q2", "1in", "1y0", "1y1", "0b0", "1zp1", "1zp2", "0r2",
    "0f1", "0f2", "0lastA", "0lastB", "0list", "F0", "1sb", "1d1", "1d2", "F1", "1q1", "N0",
    "1p1", "N1", "1p2", "1r1", "2in", "2y0", "2y1", "2zp1", "2zp2", "2sb", "1b1", "S0", "1b0",
    "1q2", "S1", "2d1", "2d2", "2q1", "2p1", "1r2", "1f1", "1f2", "1lastA", "f0", "2p2", "2r1",
    "n0", "2b1", "2b0", "2q2", "s0", "2r2", "2f1", "2f2", "2lastA", "1lastB", "2lastB", "R",
)


def kernel(
    x_hbm, cols_hbm, list_hbm, count, out_ref,
    a0, a1, a2, b0, b1, b2, q_refs, s_refs, r_refs, ca, cb, cols, pairs, idv, idx,
    loc, small, gsend, a_recv, b_recv, csend, ca_recv, cb_recv,
    q_sems, s_sems, r_sems,
):
    row, col, lay = lax.axis_index("row"), lax.axis_index("col"), lax.axis_index("layer")
    zl, y, core = col // 8, (col // 2) % 4, col % 2
    zp = 1 - zl
    a, b = (a0, a1, a2), (b0, b1, b2)
    pcol = (col + 8) % 16
    sib = col + 1 - 2 * core
    dz = 2 * zl - 1
    cidx = zl * 4 + y

    def col_of(z, yy):
        return (z * 4 + yy) * 2 + core

    rp, rm, rf = (row + 1) % 4, (row + 3) % 4, (row + 2) % 4
    rd, re = (row + 4 + dz) % 4, (row + 4 - dz) % 4
    yp, ym, yf = (y + 1) % 4, (y + 3) % 4, (y + 2) % 4
    lp, lm, lf = (lay + 1) % 4, (lay + 3) % 4, (lay + 2) % 4

    def a_part(c, h, s):
        return a[h].at[pl.ds(c * 16 + s * 8, 8)]

    def b_part(r, h, s):
        return b[h].at[pl.ds(r * 16 + s * 8, 8)]

    cols_in = pltpu.make_async_copy(cols_hbm, cols, small.at[0])
    list_in = pltpu.make_async_copy(list_hbm, pairs, small.at[1])
    own_in = []
    for h in range(3):
        rows = x_hbm.at[:, pl.ds(FIRST[h], ROWS[h])]
        own_in.append((
            pltpu.make_async_copy(rows, a[h].at[pl.ds(col * 16, 16)], loc.at[h, 0]),
            pltpu.make_async_copy(rows, b[h].at[pl.ds(row * 16, 16)], loc.at[h, 1])))
    cols_in.start()
    for pair in own_in:
        for m in pair:
            m.start()
    list_in.start()

    barrier = pltpu.get_barrier_semaphore()
    chips = [(row, ((col // 2 + k) % 8) * 2 + core, lay) for k in range(1, 8)]
    ends = [(r, col, lay) for r in (rp, rm, rf)]
    peers = chips + ends + [(row, sib, lay), (rd, pcol, lay), (row, col, lp), (row, col, lm)]
    for p in peers:
        pl.semaphore_signal(barrier, inc=1, device_id=p, device_id_type=MESH)

    for h in range(3):
        b[h][ZERO] = jnp.zeros((ROWS[h], EDGE), jnp.bfloat16)

    pl.semaphore_wait(barrier, len(peers))

    started = []

    def copy_to(src, dst, ssem, rsem, dev):
        return pltpu.make_async_remote_copy(
            src_ref=src, dst_ref=dst, send_sem=ssem, recv_sem=rsem,
            device_id=dev, device_id_type=MESH)

    def send(src, dst, ssem, rsem, dev):
        d = copy_to(src, dst, ssem, rsem, dev)
        d.start()
        started.append(d)

    to_sib = (row, sib, lay)
    to_p, to_d, to_pd, to_e = (row, pcol, lay), (rd, col, lay), (rd, pcol, lay), (re, col, lay)
    to_yp, to_ym = (row, col_of(zl, yp), lay), (row, col_of(zl, ym), lay)

    used = [0]

    def next_sem():
        used[0] += 1
        return gsend.at[used[0] - 1]

    def send_a(c, h, s, dev):
        send(a_part(c, h, s), a_part(c, h, s), next_sem(), a_recv.at[h, c, s], dev)

    def send_b(r, h, s, dev):
        send(b_part(r, h, s), b_part(r, h, s), next_sem(), b_recv.at[h, r, s], dev)

    def wait_a(c, h, s):
        copy_to(a_part(c, h, s), a_part(c, h, s), gsend.at[0], a_recv.at[h, c, s], to_sib).wait_recv()

    def wait_b(r, h, s):
        copy_to(b_part(r, h, s), b_part(r, h, s), gsend.at[0], b_recv.at[h, r, s], to_sib).wait_recv()

    def own_to(h, step):
        if step == "zp1":
            send_a(col, h, zl, to_p)
        elif step == "zp2":
            send_a(col, h, zp, to_p)
        elif step == "y0":
            send_a(col, h, 0, to_yp)
            send_a(col, h, 1, to_ym)
        elif step == "y1":
            send_a(col, h, 1, to_yp)
            send_a(col, h, 0, to_ym)
        elif step == "d1":
            send_b(row, h, zp, to_d)
        elif step == "d2":
            send_b(row, h, zl, to_d)
        elif step == "sb":
            send_a(col, h, 0, to_sib)
            send_a(col, h, 1, to_sib)
        elif step == "list":
            to_smem.wait()
        elif step == "in":
            for m in own_in[h]:
                m.wait()

    def pass_p(h, s):
        wait_a(pcol, h, s)
        send_a(pcol, h, s, to_yp)
        send_a(pcol, h, s, to_ym)
        send(a_part(pcol, h, s), b_part(row, h, s), next_sem(), b_recv.at[h, row, s], to_pd)
        send_a(pcol, h, s, to_sib)

    def pass_y(h, z):
        cm, cp = col_of(z, ym), col_of(z, yp)
        wait_a(cm, h, 0)
        send_a(cm, h, 0, to_yp)
        wait_a(cp, h, 1)
        send_a(cp, h, 1, to_ym)
        send_a(cm, h, 0, to_sib)
        send_a(cp, h, 1, to_sib)

    def rest_y(h, z):
        cm, cp = col_of(z, ym), col_of(z, yp)
        wait_a(cm, h, 1)
        send_a(cm, h, 1, to_sib)
        wait_a(cp, h, 0)
        send_a(cp, h, 0, to_sib)

    def far_y(h, z):
        cf = col_of(z, yf)
        for s in range(2):
            wait_a(cf, h, s)
            send_a(cf, h, s, to_sib)

    def far_b(h, which):
        if which == 0:
            wait_b(re, h, zp)
            send_b(re, h, zp, to_d)
        else:
            wait_b(rd, h, zl)
            send_b(rd, h, zl, to_e)

    def last_a(h):
        for z in range(2):
            for yy in range(4):
                c = (z * 4 + yy) * 2 + 1 - core
                wait_a(c, h, 0)
                wait_a(c, h, 1)

    def last_b(h):
        wait_b(re, h, zl)
        wait_b(rd, h, zp)
        wait_b(rf, h, 0)
        wait_b(rf, h, 1)

    lane = lax.broadcasted_iota(jnp.int32, (8, EDGE), 1)

    def columns():
        cols_in.wait()
        sub = lax.broadcasted_iota(jnp.int32, (8, EDGE), 0)
        for first, where in ((col * 4, ca.at[core, cidx]), (row * 4, cb.at[row])):
            vals = jnp.zeros((8, EDGE), jnp.int32)
            for s in range(2):
                for k in range(4):
                    for p in range(2):
                        vals = jnp.where((lane == first + k) & (sub == s * 2 + p), cols[s, p, k], vals)
            where[...] = vals
        for n, dev in enumerate(chips):
            send(ca.at[core, cidx], ca.at[core, cidx], csend.at[n], ca_recv.at[cidx], dev)
        for n, dev in enumerate(ends):
            send(cb.at[row], cb.at[row], csend.at[7 + n], cb_recv.at[row], dev)

    to_smem = pltpu.make_async_copy(idv, idx, small.at[2])

    def lists():
        for k in range(1, 8):
            ci = (cidx + k) % 8
            copy_to(ca.at[core, ci], ca.at[core, ci], csend.at[0], ca_recv.at[ci], to_sib).wait_recv()
        send(ca.at[core], ca.at[core], csend.at[10], ca_recv.at[8], to_sib)

    def places():
        for r in (rp, rm, rf):
            copy_to(cb.at[r], cb.at[r], csend.at[0], cb_recv.at[r], to_sib).wait_recv()
        copy_to(ca.at[1 - core], ca.at[1 - core], csend.at[0], ca_recv.at[8], to_sib).wait_recv()
        list_in.wait()
        acols = jnp.sum(ca[...].reshape(16, 8, EDGE), axis=0)
        bcols = jnp.sum(cb[...], axis=0)
        live = count[0, 0]
        for g in range(2):
            part = slice(g * EDGE, (g + 1) * EDGE)
            av = jnp.broadcast_to(pairs[0:1, part], (8, EDGE))
            bv = jnp.broadcast_to(pairs[1:2, part], (8, EDGE))
            have = jnp.take_along_axis(acols, av, axis=1, mode="promise_in_bounds")
            want = jnp.take_along_axis(bcols, bv, axis=1, mode="promise_in_bounds")
            ra, rb = av[0:1], bv[0:1]
            idv[0:1, part] = (ra >> 2) * 16 + (ra & 3) * 2
            alive = (lane[0:1] + g * EDGE) < live
            for s in range(2):
                base = (rb >> 2) * 16 + s * 8 + (rb & 3) * 2
                w0, w1 = want[s * 2 : s * 2 + 1], want[s * 2 + 1 : s * 2 + 2]
                for p in range(2):
                    q = s * 2 + p
                    h0 = have[q : q + 1]
                    at = jnp.where(h0 == w0, base, jnp.where(h0 == w1, base + 1, ZERO))
                    idv[1 + q : 2 + q, part] = jnp.where(alive, at, ZERO)
        idv[5:8, :] = jnp.zeros((3, 256), jnp.int32)
        to_smem.start()

    steps = {
        "p1": lambda h: pass_p(h, zp), "p2": lambda h: pass_p(h, zl),
        "q1": lambda h: pass_y(h, zl), "q2": lambda h: pass_y(h, zp),
        "r1": lambda h: rest_y(h, zl), "r2": lambda h: rest_y(h, zp),
        "f1": lambda h: far_y(h, zl), "f2": lambda h: far_y(h, zp),
        "b0": lambda h: far_b(h, 0), "b1": lambda h: far_b(h, 1), "lastA": last_a, "lastB": last_b,
        "cols": lambda h: columns(), "lists": lambda h: lists(), "places": lambda h: places(),
    }

    def left_of(t, h):
        u = idx[0, t]
        return jnp.concatenate([a[h][u], a[h][u + 1], a[h][u + 8], a[h][u + 9]], axis=1)

    def right_of(t, h):
        return jnp.concatenate([b[h][idx[1 + q, t]] for q in range(4)], axis=1)

    def times(left, right):
        return lax.dot_general(left, right, (((1,), (1,)), ((), ())),
                               preferred_element_type=jnp.float32)

    low = lax.broadcasted_iota(jnp.int32, (96, EDGE), 1) < HALF

    def quadrants(t):
        both = times(jnp.concatenate([left_of(t, 0), left_of(t + 1, 0)], axis=0),
                     jnp.concatenate([right_of(t, 0), right_of(t + 1, 0)], axis=0))
        return jnp.where(low[:HALF], both[:HALF], both[HALF:])

    def strips(t):
        both = times(jnp.concatenate([left_of(t, 1), left_of(t + 1, 1)], axis=0),
                     jnp.concatenate([right_of(t, 0), right_of(t + 1, 0)], axis=0))
        return jnp.where(low[:32], both[:32], both[32:])

    def whole(t):
        return times(jnp.concatenate([left_of(t, h) for h in range(3)], axis=0),
                     jnp.concatenate([right_of(t, h) for h in range(3)], axis=0))

    def rest(t):
        one, two = whole(t), whole(t + 1)
        mixed = jnp.where(low, pltpu.roll(two[:96], HALF, 1), one[:96])
        return jnp.concatenate([mixed, one[96:], two[96:]], axis=0)

    def half(v):
        return v.astype(jnp.bfloat16)

    def wide(v):
        return v.astype(jnp.float32)

    def each(n, body, unroll):
        def step(i, carry):
            for u in range(unroll):
                body(i * unroll + u)
            return carry
        lax.fori_loop(0, n // unroll, step, 0)

    def loop(n, body):
        def step(k, carry):
            body(k)
            return carry
        lax.fori_loop(0, n, step, 0)

    def next_owner(d):
        return (lay + 1 + 2 * d) % 4

    def towards(d):
        return (row, col, next_owner(d))

    class Piece:
        def __init__(self, refs, sems, value, unroll):
            self.f_out, self.f_in, self.n_out, self.n_in = refs
            self.f_send, self.f_recv, self.n_send, self.n_recv = sems
            self.value, self.unroll = value, unroll
            self.parts = self.f_send.shape[1]
            self.chunk = PAIRS // self.parts

        def f_copy(self, d, k):
            part = pl.ds(k * self.chunk, self.chunk)
            return copy_to(self.f_out.at[d, part], self.f_in.at[d, part],
                           self.f_send.at[d, k], self.f_recv.at[d, k], towards(d))

        def n_copy(self, d, g, k):
            part = pl.ds(k * self.chunk, self.chunk)
            return copy_to(self.n_out.at[d, g, part], self.n_in.at[d, g, part],
                           self.n_send.at[d, g, k], self.n_recv.at[d, g, k], towards(d))

        def far(self, k):
            def way(d):
                def body(i):
                    j = k * self.chunk + i
                    self.f_out[d, j] = half(self.value(lf * 64 + d * 32 + 2 * j))
                each(self.chunk, body, self.unroll)
                self.f_copy(d, k).start()
            loop(2, way)

        def near(self, k):
            def way(d):
                g = 1 - d
                def body(i):
                    j = k * self.chunk + i
                    self.n_out[d, g, j] = half(self.value(next_owner(d) * 64 + g * 32 + 2 * j))
                each(self.chunk, body, self.unroll)
                self.n_copy(d, g, k).start()
            loop(2, way)

        def sum(self, k):
            def way(d):
                self.f_copy(d, k).wait_recv()
                def body(i):
                    j = k * self.chunk + i
                    own = self.value(next_owner(d) * 64 + d * 32 + 2 * j)
                    self.n_out[d, d, j] = half(own + wide(self.f_in[d, j]))
                each(self.chunk, body, self.unroll)
                self.n_copy(d, d, k).start()
            loop(2, way)

        def arrived(self, g, k):
            for d in range(2):
                self.n_copy(d, g, k).wait_recv()

        def far_sent(self):
            loop(2, lambda d: loop(self.parts, lambda k: self.f_copy(d, k).wait_send()))

        def near_sent(self):
            loop(2, lambda d: loop(
                2, lambda g: loop(self.parts, lambda k: self.n_copy(d, g, k).wait_send())))

        def total(self, g, j):
            return wide(self.n_in[0, g, j]) + wide(self.n_in[1, g, j])

    corner = Piece(q_refs, q_sems, quadrants, 8)
    strip = Piece(s_refs, s_sems, strips, 8)
    remainder = Piece(r_refs, r_sems, rest, 4)

    def mine(t):
        out_ref[t] = whole(lay * 64 + t)

    def remaining():
        loop(remainder.parts, remainder.far)
        loop(remainder.parts, remainder.near)
        each(64, mine, 8)
        loop(remainder.parts, remainder.sum)

    kinds = {"F": corner.far, "N": corner.near, "S": corner.sum,
             "f": strip.far, "n": strip.near, "s": strip.sum}
    for word in ORDER:
        if word == "R":
            remaining()
        elif word[0] in kinds:
            kinds[word[0]](int(word[1:] or 0))
        elif word[1:] in steps:
            steps[word[1:]](int(word[0]))
        else:
            own_to(int(word[0]), word[1:])

    for d in started:
        d.wait_send()
    for piece in (corner, strip):
        piece.far_sent()
        piece.near_sent()
    remainder.far_sent()

    for g in range(2):
        for piece in (corner, strip):
            loop(piece.parts, lambda k: piece.arrived(g, k))

    def finish(k):
        def group(g):
            remainder.arrived(g, k)

            def body(i):
                j = k * remainder.chunk + i
                t = g * 32 + 2 * j
                first = jnp.concatenate([corner.total(g, j), strip.total(g, j)], axis=0)
                more = remainder.total(g, j)
                mixed = more[:96]
                upper, lower = pl.ds(0, 96), pl.ds(96, 32)
                out_ref[t, upper] += jnp.where(low, first, mixed)
                out_ref[t, lower] += more[96:128]
                out_ref[t + 1, upper] += pltpu.roll(jnp.where(low, mixed, first), HALF, 1)
                out_ref[t + 1, lower] += more[128:]

            each(remainder.chunk, body, 4)

        loop(2, group)

    loop(remainder.parts, finish)

    remainder.near_sent()


def on_device(x_tiles, x_cols, c_list, c_count):
    hbm = pl.BlockSpec(memory_space=pltpu.HBM)
    dma = pltpu.SemaphoreType.DMA
    bf16 = lambda *dims: pltpu.VMEM(dims + (EDGE,), jnp.bfloat16)
    ints = lambda *dims: pltpu.VMEM(dims, jnp.int32)
    buffers = lambda n: [bf16(2, PAIRS, n), bf16(2, PAIRS, n), bf16(2, 2, PAIRS, n), bf16(2, 2, PAIRS, n)]
    semaphores = lambda n: [dma((2, n)), dma((2, n)), dma((2, 2, n)), dma((2, 2, n))]
    operands = [
        pltpu.with_memory_space_constraint(v, pltpu.HBM)
        for v in (x_tiles.reshape(16, EDGE, EDGE), jnp.swapaxes(x_cols, 1, 2),
                  jnp.swapaxes(c_list[0, 0], 0, 1))
    ]
    out = pl.pallas_call(
        kernel,
        out_shape=pltpu.VMEM((64, EDGE, EDGE), jnp.float32),
        in_specs=[hbm] * 3 + [pl.BlockSpec(memory_space=pltpu.SMEM)],
        out_specs=pl.BlockSpec(memory_space=pltpu.VMEM),
        scratch_shapes=[
            *[bf16(A_UNITS, n) for n in ROWS], *[bf16(B_UNITS, n) for n in ROWS],
            buffers(64), buffers(32), buffers(160),
            ints(2, 8, 8, EDGE), ints(4, 8, EDGE),
            pltpu.SMEM((2, 2, 4), jnp.int32), ints(2, 256),
            ints(8, 256), pltpu.SMEM((8, 256), jnp.int32),
            dma((3, 2)), dma((3,)), dma((108,)), dma((3, 16, 2)), dma((3, 4, 2)),
            dma((11,)), dma((9,)), dma((4,)),
            semaphores(Q_PARTS), semaphores(S_PARTS), semaphores(R_PARTS),
        ],
        compiler_params=pltpu.CompilerParams(
            collective_id=0, has_side_effects=True, vmem_limit_bytes=40 * 1024 * 1024),
    )(*operands, c_count)
    return out[None, None]


def solution(mesh):
    return jax.shard_map(
        on_device,
        mesh=mesh,
        in_specs=(
            P("layer", ("row", "col"), None, None, None),
            P("layer", ("row", "col"), None),
            P("row", "col", None, None),
            P("row", "col"),
        ),
        out_specs=P("row", "col", "layer", None, None),
        check_vma=False,
    )
```

```python
import jax
import jax.numpy as jnp
from jax import lax
from jax.experimental import pallas as pl
from jax.experimental.pallas import tpu as pltpu
from jax.sharding import PartitionSpec as P

EDGE = 128
HALF = 64
ROWS = (64, 32, 32)
FIRST = (0, 64, 96)
A_UNITS = 256
B_UNITS = 65
ZERO = 64
PAIRS = 16
Q_PARTS, S_PARTS, R_PARTS = 2, 1, 4
MESH = pl.DeviceIdType.MESH
ORDER = (
    "0in", "0zp1", "0zp2", "0y0", "0y1", "0sb", "0d1", "0cols", "0q1", "0p1", "0d2", "0lists",
    "0p2", "0r1", "0b1", "0b0", "0f1", "0places", "0q2", "1in", "1y0", "1y1", "1zp1", "1zp2",
    "0r2", "0f2", "0lastA", "0lastB", "0list", "F0", "1sb", "1d1", "1d2", "F1", "1q1", "N0",
    "1p1", "N1", "1p2", "1r1", "2in", "2y0", "2y1", "2zp1", "2zp2", "2sb", "1b1", "S0", "1b0",
    "1q2", "S1", "2d1", "2d2", "2q1", "2p1", "1r2", "1f1", "1f2", "1lastA", "f0", "2p2", "2r1",
    "n0", "2b1", "2b0", "2q2", "s0", "2r2", "2f1", "2f2", "2lastA", "1lastB", "2lastB", "R",
)


def kernel(
    x_hbm, cols_hbm, list_hbm, count, out_ref,
    a0, a1, a2, b0, b1, b2, q_refs, s_refs, r_refs, ca, cb, cols, pairs, idv, idx,
    loc, small, gsend, a_recv, b_recv, csend, ca_recv, cb_recv,
    q_sems, s_sems, r_sems,
):
    row, col, lay = lax.axis_index("row"), lax.axis_index("col"), lax.axis_index("layer")
    zl, y, core = col // 8, (col // 2) % 4, col % 2
    zp = 1 - zl
    a, b = (a0, a1, a2), (b0, b1, b2)
    pcol = (col + 8) % 16
    sib = col + 1 - 2 * core
    dz = 2 * zl - 1
    cidx = zl * 4 + y

    def col_of(z, yy):
        return (z * 4 + yy) * 2 + core

    rp, rm, rf = (row + 1) % 4, (row + 3) % 4, (row + 2) % 4
    rd, re = (row + 4 + dz) % 4, (row + 4 - dz) % 4
    yp, ym, yf = (y + 1) % 4, (y + 3) % 4, (y + 2) % 4
    lp, lm, lf = (lay + 1) % 4, (lay + 3) % 4, (lay + 2) % 4

    def a_part(c, h, s):
        return a[h].at[pl.ds(c * 16 + s * 8, 8)]

    def b_part(r, h, s):
        return b[h].at[pl.ds(r * 16 + s * 8, 8)]

    cols_in = pltpu.make_async_copy(cols_hbm, cols, small.at[0])
    list_in = pltpu.make_async_copy(list_hbm, pairs, small.at[1])
    own_in = []
    for h in range(3):
        rows = x_hbm.at[:, pl.ds(FIRST[h], ROWS[h])]
        own_in.append((
            pltpu.make_async_copy(rows, a[h].at[pl.ds(col * 16, 16)], loc.at[h, 0]),
            pltpu.make_async_copy(rows, b[h].at[pl.ds(row * 16, 16)], loc.at[h, 1])))
    cols_in.start()
    for pair in own_in:
        for m in pair:
            m.start()
    list_in.start()

    barrier = pltpu.get_barrier_semaphore()
    chips = [(row, ((col // 2 + k) % 8) * 2 + core, lay) for k in range(1, 8)]
    ends = [(r, col, lay) for r in (rp, rm, rf)]
    peers = chips + ends + [(row, sib, lay), (rd, pcol, lay), (row, col, lp), (row, col, lm)]
    for p in peers:
        pl.semaphore_signal(barrier, inc=1, device_id=p, device_id_type=MESH)

    for h in range(3):
        b[h][ZERO] = jnp.zeros((ROWS[h], EDGE), jnp.bfloat16)

    pl.semaphore_wait(barrier, len(peers))

    started = []

    def copy_to(src, dst, ssem, rsem, dev):
        return pltpu.make_async_remote_copy(
            src_ref=src, dst_ref=dst, send_sem=ssem, recv_sem=rsem,
            device_id=dev, device_id_type=MESH)

    def send(src, dst, ssem, rsem, dev):
        d = copy_to(src, dst, ssem, rsem, dev)
        d.start()
        started.append(d)

    to_sib = (row, sib, lay)
    to_p, to_d, to_pd, to_e = (row, pcol, lay), (rd, col, lay), (rd, pcol, lay), (re, col, lay)
    to_yp, to_ym = (row, col_of(zl, yp), lay), (row, col_of(zl, ym), lay)

    used = [0]

    def next_sem():
        used[0] += 1
        return gsend.at[used[0] - 1]

    def send_a(c, h, s, dev):
        send(a_part(c, h, s), a_part(c, h, s), next_sem(), a_recv.at[h, c, s], dev)

    def send_b(r, h, s, dev):
        send(b_part(r, h, s), b_part(r, h, s), next_sem(), b_recv.at[h, r, s], dev)

    def wait_a(c, h, s):
        copy_to(a_part(c, h, s), a_part(c, h, s), gsend.at[0], a_recv.at[h, c, s], to_sib).wait_recv()

    def wait_b(r, h, s):
        copy_to(b_part(r, h, s), b_part(r, h, s), gsend.at[0], b_recv.at[h, r, s], to_sib).wait_recv()

    def own_to(h, step):
        if step == "zp1":
            send_a(col, h, zl, to_p)
        elif step == "zp2":
            send_a(col, h, zp, to_p)
        elif step == "y0":
            send_a(col, h, 0, to_yp)
            send_a(col, h, 1, to_ym)
        elif step == "y1":
            send_a(col, h, 1, to_yp)
            send_a(col, h, 0, to_ym)
        elif step == "d1":
            send_b(row, h, zp, to_d)
        elif step == "d2":
            send_b(row, h, zl, to_d)
        elif step == "sb":
            send_a(col, h, 0, to_sib)
            send_a(col, h, 1, to_sib)
        elif step == "list":
            to_smem.wait()
        elif step == "in":
            for m in own_in[h]:
                m.wait()

    def pass_p(h, s):
        wait_a(pcol, h, s)
        send_a(pcol, h, s, to_yp)
        send_a(pcol, h, s, to_ym)
        send(a_part(pcol, h, s), b_part(row, h, s), next_sem(), b_recv.at[h, row, s], to_pd)
        send_a(pcol, h, s, to_sib)

    def pass_y(h, z):
        cm, cp = col_of(z, ym), col_of(z, yp)
        wait_a(cm, h, 0)
        send_a(cm, h, 0, to_yp)
        wait_a(cp, h, 1)
        send_a(cp, h, 1, to_ym)
        send_a(cm, h, 0, to_sib)
        send_a(cp, h, 1, to_sib)

    def rest_y(h, z):
        cm, cp = col_of(z, ym), col_of(z, yp)
        wait_a(cm, h, 1)
        send_a(cm, h, 1, to_sib)
        wait_a(cp, h, 0)
        send_a(cp, h, 0, to_sib)

    def far_y(h, z):
        cf = col_of(z, yf)
        for s in range(2):
            wait_a(cf, h, s)
            send_a(cf, h, s, to_sib)

    def far_b(h, which):
        if which == 0:
            wait_b(re, h, zp)
            send_b(re, h, zp, to_d)
        else:
            wait_b(rd, h, zl)
            send_b(rd, h, zl, to_e)

    def last_a(h):
        for z in range(2):
            for yy in range(4):
                c = (z * 4 + yy) * 2 + 1 - core
                wait_a(c, h, 0)
                wait_a(c, h, 1)

    def last_b(h):
        wait_b(re, h, zl)
        wait_b(rd, h, zp)
        wait_b(rf, h, 0)
        wait_b(rf, h, 1)

    lane = lax.broadcasted_iota(jnp.int32, (8, EDGE), 1)

    def columns():
        cols_in.wait()
        sub = lax.broadcasted_iota(jnp.int32, (8, EDGE), 0)
        for first, where in ((col * 4, ca.at[core, cidx]), (row * 4, cb.at[row])):
            vals = jnp.zeros((8, EDGE), jnp.int32)
            for s in range(2):
                for k in range(4):
                    for p in range(2):
                        vals = jnp.where((lane == first + k) & (sub == s * 2 + p), cols[s, p, k], vals)
            where[...] = vals
        for n, dev in enumerate(chips):
            send(ca.at[core, cidx], ca.at[core, cidx], csend.at[n], ca_recv.at[cidx], dev)
        for n, dev in enumerate(ends):
            send(cb.at[row], cb.at[row], csend.at[7 + n], cb_recv.at[row], dev)

    to_smem = pltpu.make_async_copy(idv, idx, small.at[2])

    def lists():
        for k in range(1, 8):
            ci = (cidx + k) % 8
            copy_to(ca.at[core, ci], ca.at[core, ci], csend.at[0], ca_recv.at[ci], to_sib).wait_recv()
        send(ca.at[core], ca.at[core], csend.at[10], ca_recv.at[8], to_sib)

    def places():
        for r in (rp, rm, rf):
            copy_to(cb.at[r], cb.at[r], csend.at[0], cb_recv.at[r], to_sib).wait_recv()
        copy_to(ca.at[1 - core], ca.at[1 - core], csend.at[0], ca_recv.at[8], to_sib).wait_recv()
        list_in.wait()
        acols = jnp.sum(ca[...].reshape(16, 8, EDGE), axis=0)
        bcols = jnp.sum(cb[...], axis=0)
        live = count[0, 0]
        for g in range(2):
            part = slice(g * EDGE, (g + 1) * EDGE)
            av = jnp.broadcast_to(pairs[0:1, part], (8, EDGE))
            bv = jnp.broadcast_to(pairs[1:2, part], (8, EDGE))
            have = jnp.take_along_axis(acols, av, axis=1, mode="promise_in_bounds")
            want = jnp.take_along_axis(bcols, bv, axis=1, mode="promise_in_bounds")
            ra, rb = av[0:1], bv[0:1]
            idv[0:1, part] = (ra >> 2) * 16 + (ra & 3) * 2
            alive = (lane[0:1] + g * EDGE) < live
            for s in range(2):
                base = (rb >> 2) * 16 + s * 8 + (rb & 3) * 2
                w0, w1 = want[s * 2 : s * 2 + 1], want[s * 2 + 1 : s * 2 + 2]
                for p in range(2):
                    q = s * 2 + p
                    h0 = have[q : q + 1]
                    at = jnp.where(h0 == w0, base, jnp.where(h0 == w1, base + 1, ZERO))
                    idv[1 + q : 2 + q, part] = jnp.where(alive, at, ZERO)
        idv[5:8, :] = jnp.zeros((3, 256), jnp.int32)
        to_smem.start()

    steps = {
        "p1": lambda h: pass_p(h, zp), "p2": lambda h: pass_p(h, zl),
        "q1": lambda h: pass_y(h, zl), "q2": lambda h: pass_y(h, zp),
        "r1": lambda h: rest_y(h, zl), "r2": lambda h: rest_y(h, zp),
        "f1": lambda h: far_y(h, zl), "f2": lambda h: far_y(h, zp),
        "b0": lambda h: far_b(h, 0), "b1": lambda h: far_b(h, 1), "lastA": last_a, "lastB": last_b,
        "cols": lambda h: columns(), "lists": lambda h: lists(), "places": lambda h: places(),
    }

    def left_of(t, h):
        u = idx[0, t]
        return jnp.concatenate([a[h][u], a[h][u + 1], a[h][u + 8], a[h][u + 9]], axis=1)

    def right_of(t, h):
        return jnp.concatenate([b[h][idx[1 + q, t]] for q in range(4)], axis=1)

    def times(left, right):
        return lax.dot_general(left, right, (((1,), (1,)), ((), ())),
                               preferred_element_type=jnp.float32)

    low = lax.broadcasted_iota(jnp.int32, (96, EDGE), 1) < HALF

    def quadrants(t):
        both = times(jnp.concatenate([left_of(t, 0), left_of(t + 1, 0)], axis=0),
                     jnp.concatenate([right_of(t, 0), right_of(t + 1, 0)], axis=0))
        return jnp.where(low[:HALF], both[:HALF], both[HALF:])

    def strips(t):
        both = times(jnp.concatenate([left_of(t, 1), left_of(t + 1, 1)], axis=0),
                     jnp.concatenate([right_of(t, 0), right_of(t + 1, 0)], axis=0))
        return jnp.where(low[:32], both[:32], both[32:])

    def whole(t):
        return times(jnp.concatenate([left_of(t, h) for h in range(3)], axis=0),
                     jnp.concatenate([right_of(t, h) for h in range(3)], axis=0))

    def rest(t):
        one, two = whole(t), whole(t + 1)
        mixed = jnp.where(low, pltpu.roll(two[:96], HALF, 1), one[:96])
        return jnp.concatenate([mixed, one[96:], two[96:]], axis=0)

    def half(v):
        return v.astype(jnp.bfloat16)

    def wide(v):
        return v.astype(jnp.float32)

    def each(n, body, unroll):
        def step(i, carry):
            for u in range(unroll):
                body(i * unroll + u)
            return carry
        lax.fori_loop(0, n // unroll, step, 0)

    def loop(n, body):
        def step(k, carry):
            body(k)
            return carry
        lax.fori_loop(0, n, step, 0)

    def next_owner(d):
        return (lay + 1 + 2 * d) % 4

    def towards(d):
        return (row, col, next_owner(d))

    class Piece:
        def __init__(self, refs, sems, value, unroll):
            self.f_out, self.f_in, self.n_out, self.n_in = refs
            self.f_send, self.f_recv, self.n_send, self.n_recv = sems
            self.value, self.unroll = value, unroll
            self.parts = self.f_send.shape[1]
            self.chunk = PAIRS // self.parts

        def f_copy(self, d, k):
            part = pl.ds(k * self.chunk, self.chunk)
            return copy_to(self.f_out.at[d, part], self.f_in.at[d, part],
                           self.f_send.at[d, k], self.f_recv.at[d, k], towards(d))

        def n_copy(self, d, g, k):
            part = pl.ds(k * self.chunk, self.chunk)
            return copy_to(self.n_out.at[d, g, part], self.n_in.at[d, g, part],
                           self.n_send.at[d, g, k], self.n_recv.at[d, g, k], towards(d))

        def far(self, k):
            def way(d):
                def body(i):
                    j = k * self.chunk + i
                    self.f_out[d, j] = half(self.value(lf * 64 + d * 32 + 2 * j))
                each(self.chunk, body, self.unroll)
                self.f_copy(d, k).start()
            loop(2, way)

        def near(self, k):
            def way(d):
                g = 1 - d
                def body(i):
                    j = k * self.chunk + i
                    self.n_out[d, g, j] = half(self.value(next_owner(d) * 64 + g * 32 + 2 * j))
                each(self.chunk, body, self.unroll)
                self.n_copy(d, g, k).start()
            loop(2, way)

        def sum(self, k):
            def way(d):
                self.f_copy(d, k).wait_recv()
                def body(i):
                    j = k * self.chunk + i
                    own = self.value(next_owner(d) * 64 + d * 32 + 2 * j)
                    self.n_out[d, d, j] = half(own + wide(self.f_in[d, j]))
                each(self.chunk, body, self.unroll)
                self.n_copy(d, d, k).start()
            loop(2, way)

        def arrived(self, g, k):
            for d in range(2):
                self.n_copy(d, g, k).wait_recv()

        def far_sent(self):
            loop(2, lambda d: loop(self.parts, lambda k: self.f_copy(d, k).wait_send()))

        def near_sent(self):
            loop(2, lambda d: loop(
                2, lambda g: loop(self.parts, lambda k: self.n_copy(d, g, k).wait_send())))

        def total(self, g, j):
            return wide(self.n_in[0, g, j]) + wide(self.n_in[1, g, j])

    corner = Piece(q_refs, q_sems, quadrants, 8)
    strip = Piece(s_refs, s_sems, strips, 8)
    remainder = Piece(r_refs, r_sems, rest, 4)

    def mine(t):
        out_ref[t] = whole(lay * 64 + t)

    def remaining():
        loop(remainder.parts, remainder.far)
        loop(remainder.parts, remainder.near)
        each(64, mine, 8)
        loop(remainder.parts, remainder.sum)

    kinds = {"F": corner.far, "N": corner.near, "S": corner.sum,
             "f": strip.far, "n": strip.near, "s": strip.sum}
    for word in ORDER:
        if word == "R":
            remaining()
        elif word[0] in kinds:
            kinds[word[0]](int(word[1:] or 0))
        elif word[1:] in steps:
            steps[word[1:]](int(word[0]))
        else:
            own_to(int(word[0]), word[1:])

    for d in started:
        d.wait_send()
    for piece in (corner, strip):
        piece.far_sent()
        piece.near_sent()
    remainder.far_sent()

    for g in range(2):
        for piece in (corner, strip):
            loop(piece.parts, lambda k: piece.arrived(g, k))

    def finish(k):
        def group(g):
            remainder.arrived(g, k)

            def body(i):
                j = k * remainder.chunk + i
                t = g * 32 + 2 * j
                first = jnp.concatenate([corner.total(g, j), strip.total(g, j)], axis=0)
                more = remainder.total(g, j)
                mixed = more[:96]
                upper, lower = pl.ds(0, 96), pl.ds(96, 32)
                out_ref[t, upper] += jnp.where(low, first, mixed)
                out_ref[t, lower] += more[96:128]
                out_ref[t + 1, upper] += pltpu.roll(jnp.where(low, mixed, first), HALF, 1)
                out_ref[t + 1, lower] += more[128:]

            each(remainder.chunk, body, 4)

        loop(2, group)

    loop(remainder.parts, finish)

    remainder.near_sent()


def on_device(x_tiles, x_cols, c_list, c_count):
    hbm = pl.BlockSpec(memory_space=pltpu.HBM)
    dma = pltpu.SemaphoreType.DMA
    bf16 = lambda *dims: pltpu.VMEM(dims + (EDGE,), jnp.bfloat16)
    ints = lambda *dims: pltpu.VMEM(dims, jnp.int32)
    buffers = lambda n: [bf16(2, PAIRS, n), bf16(2, PAIRS, n), bf16(2, 2, PAIRS, n), bf16(2, 2, PAIRS, n)]
    semaphores = lambda n: [dma((2, n)), dma((2, n)), dma((2, 2, n)), dma((2, 2, n))]
    operands = [
        pltpu.with_memory_space_constraint(v, pltpu.HBM)
        for v in (x_tiles.reshape(16, EDGE, EDGE), jnp.swapaxes(x_cols, 1, 2),
                  jnp.swapaxes(c_list[0, 0], 0, 1))
    ]
    out = pl.pallas_call(
        kernel,
        out_shape=pltpu.VMEM((64, EDGE, EDGE), jnp.float32),
        in_specs=[hbm] * 3 + [pl.BlockSpec(memory_space=pltpu.SMEM)],
        out_specs=pl.BlockSpec(memory_space=pltpu.VMEM),
        scratch_shapes=[
            *[bf16(A_UNITS, n) for n in ROWS], *[bf16(B_UNITS, n) for n in ROWS],
            buffers(64), buffers(32), buffers(160),
            ints(2, 8, 8, EDGE), ints(4, 8, EDGE),
            pltpu.SMEM((2, 2, 4), jnp.int32), ints(2, 256),
            ints(8, 256), pltpu.SMEM((8, 256), jnp.int32),
            dma((3, 2)), dma((3,)), dma((108,)), dma((3, 16, 2)), dma((3, 4, 2)),
            dma((11,)), dma((9,)), dma((4,)),
            semaphores(Q_PARTS), semaphores(S_PARTS), semaphores(R_PARTS),
        ],
        compiler_params=pltpu.CompilerParams(
            collective_id=0, has_side_effects=True, vmem_limit_bytes=40 * 1024 * 1024),
    )(*operands, c_count)
    return out[None, None]


def solution(mesh):
    return jax.shard_map(
        on_device,
        mesh=mesh,
        in_specs=(
            P("layer", ("row", "col"), None, None, None),
            P("layer", ("row", "col"), None),
            P("row", "col", None, None),
            P("row", "col"),
        ),
        out_specs=P("row", "col", "layer", None, None),
        check_vma=False,
    )
```

```python
import jax
import jax.numpy as jnp
from jax import lax
from jax.experimental import pallas as pl
from jax.experimental.pallas import tpu as pltpu
from jax.sharding import PartitionSpec as P

EDGE = 128
HALF = 64
ROWS = (64, 32, 32)
FIRST = (0, 64, 96)
A_UNITS = 256
B_UNITS = 65
ZERO = 64
PAIRS = 16
Q_PARTS, S_PARTS, R_PARTS = 2, 1, 4
MESH = pl.DeviceIdType.MESH
ORDER = (
    "0in", "0zp1", "0zp2", "0y0", "0y1", "0sb", "0d1", "0cols", "0q1", "0p1", "0d2", "0lists",
    "0p2", "0r1", "0b1", "0b0", "0f1", "0places", "0q2", "1in", "1y0", "1y1", "1zp1", "1zp2",
    "0r2", "0f2", "0lastA", "0lastB", "0list", "F0", "1sb", "1d1", "1d2", "F1", "1q1", "N0",
    "1p1", "N1", "1p2", "1r1", "2in", "2y0", "2y1", "2zp1", "2zp2", "2sb", "1b0", "S0", "1b1",
    "1q2", "S1", "2d1", "2d2", "2q1", "2p1", "1r2", "1f1", "1f2", "1lastA", "f0", "2p2", "2r1",
    "n0", "2b0", "2b1", "2q2", "s0", "2r2", "2f1", "2f2", "2lastA", "1lastB", "2lastB", "R",
)


def kernel(
    x_hbm, cols_hbm, list_hbm, count, out_ref,
    a0, a1, a2, b0, b1, b2, q_refs, s_refs, r_refs, ca, cb, cols, pairs, idv, idx,
    loc, small, gsend, a_recv, b_recv, csend, ca_recv, cb_recv,
    q_sems, s_sems, r_sems,
):
    row, col, lay = lax.axis_index("row"), lax.axis_index("col"), lax.axis_index("layer")
    zl, y, core = col // 8, (col // 2) % 4, col % 2
    zp = 1 - zl
    a, b = (a0, a1, a2), (b0, b1, b2)
    pcol = (col + 8) % 16
    sib = col + 1 - 2 * core
    dz = 2 * zl - 1
    cidx = zl * 4 + y

    def col_of(z, yy):
        return (z * 4 + yy) * 2 + core

    rp, rm, rf = (row + 1) % 4, (row + 3) % 4, (row + 2) % 4
    rd, re = (row + 4 + dz) % 4, (row + 4 - dz) % 4
    yp, ym, yf = (y + 1) % 4, (y + 3) % 4, (y + 2) % 4
    lp, lm, lf = (lay + 1) % 4, (lay + 3) % 4, (lay + 2) % 4

    def a_part(c, h, s):
        return a[h].at[pl.ds(c * 16 + s * 8, 8)]

    def b_part(r, h, s):
        return b[h].at[pl.ds(r * 16 + s * 8, 8)]

    cols_in = pltpu.make_async_copy(cols_hbm, cols, small.at[0])
    list_in = pltpu.make_async_copy(list_hbm, pairs, small.at[1])
    own_in = []
    for h in range(3):
        rows = x_hbm.at[:, pl.ds(FIRST[h], ROWS[h])]
        own_in.append((
            pltpu.make_async_copy(rows, a[h].at[pl.ds(col * 16, 16)], loc.at[h, 0]),
            pltpu.make_async_copy(rows, b[h].at[pl.ds(row * 16, 16)], loc.at[h, 1])))
    cols_in.start()
    for pair in own_in:
        for m in pair:
            m.start()
    list_in.start()

    barrier = pltpu.get_barrier_semaphore()
    chips = [(row, ((col // 2 + k) % 8) * 2 + core, lay) for k in range(1, 8)]
    ends = [(r, col, lay) for r in (rp, rm, rf)]
    peers = chips + ends + [(row, sib, lay), (rd, pcol, lay), (row, col, lp), (row, col, lm)]
    for p in peers:
        pl.semaphore_signal(barrier, inc=1, device_id=p, device_id_type=MESH)

    for h in range(3):
        b[h][ZERO] = jnp.zeros((ROWS[h], EDGE), jnp.bfloat16)

    pl.semaphore_wait(barrier, len(peers))

    started = []

    def copy_to(src, dst, ssem, rsem, dev):
        return pltpu.make_async_remote_copy(
            src_ref=src, dst_ref=dst, send_sem=ssem, recv_sem=rsem,
            device_id=dev, device_id_type=MESH)

    def send(src, dst, ssem, rsem, dev):
        d = copy_to(src, dst, ssem, rsem, dev)
        d.start()
        started.append(d)

    to_sib = (row, sib, lay)
    to_p, to_d, to_pd, to_e = (row, pcol, lay), (rd, col, lay), (rd, pcol, lay), (re, col, lay)
    to_yp, to_ym = (row, col_of(zl, yp), lay), (row, col_of(zl, ym), lay)

    used = [0]

    def next_sem():
        used[0] += 1
        return gsend.at[used[0] - 1]

    def send_a(c, h, s, dev):
        send(a_part(c, h, s), a_part(c, h, s), next_sem(), a_recv.at[h, c, s], dev)

    def send_b(r, h, s, dev):
        send(b_part(r, h, s), b_part(r, h, s), next_sem(), b_recv.at[h, r, s], dev)

    def wait_a(c, h, s):
        copy_to(a_part(c, h, s), a_part(c, h, s), gsend.at[0], a_recv.at[h, c, s], to_sib).wait_recv()

    def wait_b(r, h, s):
        copy_to(b_part(r, h, s), b_part(r, h, s), gsend.at[0], b_recv.at[h, r, s], to_sib).wait_recv()

    def own_to(h, step):
        if step == "zp1":
            send_a(col, h, zl, to_p)
        elif step == "zp2":
            send_a(col, h, zp, to_p)
        elif step == "y0":
            send_a(col, h, 0, to_yp)
            send_a(col, h, 1, to_ym)
        elif step == "y1":
            send_a(col, h, 1, to_yp)
            send_a(col, h, 0, to_ym)
        elif step == "d1":
            send_b(row, h, zp, to_d)
        elif step == "d2":
            send_b(row, h, zl, to_d)
        elif step == "sb":
            send_a(col, h, 0, to_sib)
            send_a(col, h, 1, to_sib)
        elif step == "list":
            to_smem.wait()
        elif step == "in":
            for m in own_in[h]:
                m.wait()

    def pass_p(h, s):
        wait_a(pcol, h, s)
        send_a(pcol, h, s, to_yp)
        send_a(pcol, h, s, to_ym)
        send(a_part(pcol, h, s), b_part(row, h, s), next_sem(), b_recv.at[h, row, s], to_pd)
        send_a(pcol, h, s, to_sib)

    def pass_y(h, z):
        cm, cp = col_of(z, ym), col_of(z, yp)
        wait_a(cm, h, 0)
        send_a(cm, h, 0, to_yp)
        wait_a(cp, h, 1)
        send_a(cp, h, 1, to_ym)
        send_a(cm, h, 0, to_sib)
        send_a(cp, h, 1, to_sib)

    def rest_y(h, z):
        cm, cp = col_of(z, ym), col_of(z, yp)
        wait_a(cm, h, 1)
        send_a(cm, h, 1, to_sib)
        wait_a(cp, h, 0)
        send_a(cp, h, 0, to_sib)

    def far_y(h, z):
        cf = col_of(z, yf)
        for s in range(2):
            wait_a(cf, h, s)
            send_a(cf, h, s, to_sib)

    def far_b(h, which):
        if which == 0:
            wait_b(re, h, zp)
            send_b(re, h, zp, to_d)
        else:
            wait_b(rd, h, zl)
            send_b(rd, h, zl, to_e)

    def last_a(h):
        for z in range(2):
            for yy in range(4):
                c = (z * 4 + yy) * 2 + 1 - core
                wait_a(c, h, 0)
                wait_a(c, h, 1)

    def last_b(h):
        wait_b(re, h, zl)
        wait_b(rd, h, zp)
        wait_b(rf, h, 0)
        wait_b(rf, h, 1)

    lane = lax.broadcasted_iota(jnp.int32, (8, EDGE), 1)

    def columns():
        cols_in.wait()
        sub = lax.broadcasted_iota(jnp.int32, (8, EDGE), 0)
        for first, where in ((col * 4, ca.at[core, cidx]), (row * 4, cb.at[row])):
            vals = jnp.zeros((8, EDGE), jnp.int32)
            for s in range(2):
                for k in range(4):
                    for p in range(2):
                        vals = jnp.where((lane == first + k) & (sub == s * 2 + p), cols[s, p, k], vals)
            where[...] = vals
        for n, dev in enumerate(chips):
            send(ca.at[core, cidx], ca.at[core, cidx], csend.at[n], ca_recv.at[cidx], dev)
        for n, dev in enumerate(ends):
            send(cb.at[row], cb.at[row], csend.at[7 + n], cb_recv.at[row], dev)

    to_smem = pltpu.make_async_copy(idv, idx, small.at[2])

    def lists():
        for k in range(1, 8):
            ci = (cidx + k) % 8
            copy_to(ca.at[core, ci], ca.at[core, ci], csend.at[0], ca_recv.at[ci], to_sib).wait_recv()
        send(ca.at[core], ca.at[core], csend.at[10], ca_recv.at[8], to_sib)

    def places():
        for r in (rp, rm, rf):
            copy_to(cb.at[r], cb.at[r], csend.at[0], cb_recv.at[r], to_sib).wait_recv()
        copy_to(ca.at[1 - core], ca.at[1 - core], csend.at[0], ca_recv.at[8], to_sib).wait_recv()
        list_in.wait()
        acols = jnp.sum(ca[...].reshape(16, 8, EDGE), axis=0)
        bcols = jnp.sum(cb[...], axis=0)
        live = count[0, 0]
        for g in range(2):
            part = slice(g * EDGE, (g + 1) * EDGE)
            av = jnp.broadcast_to(pairs[0:1, part], (8, EDGE))
            bv = jnp.broadcast_to(pairs[1:2, part], (8, EDGE))
            have = jnp.take_along_axis(acols, av, axis=1, mode="promise_in_bounds")
            want = jnp.take_along_axis(bcols, bv, axis=1, mode="promise_in_bounds")
            ra, rb = av[0:1], bv[0:1]
            idv[0:1, part] = (ra >> 2) * 16 + (ra & 3) * 2
            alive = (lane[0:1] + g * EDGE) < live
            for s in range(2):
                base = (rb >> 2) * 16 + s * 8 + (rb & 3) * 2
                w0, w1 = want[s * 2 : s * 2 + 1], want[s * 2 + 1 : s * 2 + 2]
                for p in range(2):
                    q = s * 2 + p
                    h0 = have[q : q + 1]
                    at = jnp.where(h0 == w0, base, jnp.where(h0 == w1, base + 1, ZERO))
                    idv[1 + q : 2 + q, part] = jnp.where(alive, at, ZERO)
        idv[5:8, :] = jnp.zeros((3, 256), jnp.int32)
        to_smem.start()

    steps = {
        "p1": lambda h: pass_p(h, zp), "p2": lambda h: pass_p(h, zl),
        "q1": lambda h: pass_y(h, zl), "q2": lambda h: pass_y(h, zp),
        "r1": lambda h: rest_y(h, zl), "r2": lambda h: rest_y(h, zp),
        "f1": lambda h: far_y(h, zl), "f2": lambda h: far_y(h, zp),
        "b0": lambda h: far_b(h, 0), "b1": lambda h: far_b(h, 1), "lastA": last_a, "lastB": last_b,
        "cols": lambda h: columns(), "lists": lambda h: lists(), "places": lambda h: places(),
    }

    def left_of(t, h):
        u = idx[0, t]
        return jnp.concatenate([a[h][u], a[h][u + 1], a[h][u + 8], a[h][u + 9]], axis=1)

    def right_of(t, h):
        return jnp.concatenate([b[h][idx[1 + q, t]] for q in range(4)], axis=1)

    def times(left, right):
        return lax.dot_general(left, right, (((1,), (1,)), ((), ())),
                               preferred_element_type=jnp.float32)

    low = lax.broadcasted_iota(jnp.int32, (96, EDGE), 1) < HALF

    def quadrants(t):
        both = times(jnp.concatenate([left_of(t, 0), left_of(t + 1, 0)], axis=0),
                     jnp.concatenate([right_of(t, 0), right_of(t + 1, 0)], axis=0))
        return jnp.where(low[:HALF], both[:HALF], both[HALF:])

    def strips(t):
        both = times(jnp.concatenate([left_of(t, 1), left_of(t + 1, 1)], axis=0),
                     jnp.concatenate([right_of(t, 0), right_of(t + 1, 0)], axis=0))
        return jnp.where(low[:32], both[:32], both[32:])

    def whole(t):
        return times(jnp.concatenate([left_of(t, h) for h in range(3)], axis=0),
                     jnp.concatenate([right_of(t, h) for h in range(3)], axis=0))

    def rest(t):
        one, two = whole(t), whole(t + 1)
        mixed = jnp.where(low, pltpu.roll(two[:96], HALF, 1), one[:96])
        return jnp.concatenate([mixed, one[96:], two[96:]], axis=0)

    def half(v):
        return v.astype(jnp.bfloat16)

    def wide(v):
        return v.astype(jnp.float32)

    def each(n, body, unroll):
        def step(i, carry):
            for u in range(unroll):
                body(i * unroll + u)
            return carry
        lax.fori_loop(0, n // unroll, step, 0)

    def loop(n, body):
        def step(k, carry):
            body(k)
            return carry
        lax.fori_loop(0, n, step, 0)

    def next_owner(d):
        return (lay + 1 + 2 * d) % 4

    def towards(d):
        return (row, col, next_owner(d))

    class Piece:
        def __init__(self, refs, sems, value, unroll):
            self.f_out, self.f_in, self.n_out, self.n_in = refs
            self.f_send, self.f_recv, self.n_send, self.n_recv = sems
            self.value, self.unroll = value, unroll
            self.parts = self.f_send.shape[1]
            self.chunk = PAIRS // self.parts

        def f_copy(self, d, k):
            part = pl.ds(k * self.chunk, self.chunk)
            return copy_to(self.f_out.at[d, part], self.f_in.at[d, part],
                           self.f_send.at[d, k], self.f_recv.at[d, k], towards(d))

        def n_copy(self, d, g, k):
            part = pl.ds(k * self.chunk, self.chunk)
            return copy_to(self.n_out.at[d, g, part], self.n_in.at[d, g, part],
                           self.n_send.at[d, g, k], self.n_recv.at[d, g, k], towards(d))

        def far(self, k):
            def way(d):
                def body(i):
                    j = k * self.chunk + i
                    self.f_out[d, j] = half(self.value(lf * 64 + d * 32 + 2 * j))
                each(self.chunk, body, self.unroll)
                self.f_copy(d, k).start()
            loop(2, way)

        def near(self, k):
            def way(d):
                g = 1 - d
                def body(i):
                    j = k * self.chunk + i
                    self.n_out[d, g, j] = half(self.value(next_owner(d) * 64 + g * 32 + 2 * j))
                each(self.chunk, body, self.unroll)
                self.n_copy(d, g, k).start()
            loop(2, way)

        def sum(self, k):
            def way(d):
                self.f_copy(d, k).wait_recv()
                def body(i):
                    j = k * self.chunk + i
                    own = self.value(next_owner(d) * 64 + d * 32 + 2 * j)
                    self.n_out[d, d, j] = half(own + wide(self.f_in[d, j]))
                each(self.chunk, body, self.unroll)
                self.n_copy(d, d, k).start()
            loop(2, way)

        def arrived(self, g, k):
            for d in range(2):
                self.n_copy(d, g, k).wait_recv()

        def far_sent(self):
            loop(2, lambda d: loop(self.parts, lambda k: self.f_copy(d, k).wait_send()))

        def near_sent(self):
            loop(2, lambda d: loop(
                2, lambda g: loop(self.parts, lambda k: self.n_copy(d, g, k).wait_send())))

        def total(self, g, j):
            return wide(self.n_in[0, g, j]) + wide(self.n_in[1, g, j])

    corner = Piece(q_refs, q_sems, quadrants, 8)
    strip = Piece(s_refs, s_sems, strips, 8)
    remainder = Piece(r_refs, r_sems, rest, 4)

    def mine(t):
        out_ref[t] = whole(lay * 64 + t)

    def remaining():
        loop(remainder.parts, remainder.far)
        loop(remainder.parts, remainder.near)
        each(64, mine, 8)
        loop(remainder.parts, remainder.sum)

    kinds = {"F": corner.far, "N": corner.near, "S": corner.sum,
             "f": strip.far, "n": strip.near, "s": strip.sum}
    for word in ORDER:
        if word == "R":
            remaining()
        elif word[0] in kinds:
            kinds[word[0]](int(word[1:] or 0))
        elif word[1:] in steps:
            steps[word[1:]](int(word[0]))
        else:
            own_to(int(word[0]), word[1:])

    for d in started:
        d.wait_send()
    for piece in (corner, strip):
        piece.far_sent()
        piece.near_sent()
    remainder.far_sent()

    for g in range(2):
        for piece in (corner, strip):
            loop(piece.parts, lambda k: piece.arrived(g, k))

    def finish(k):
        def group(g):
            remainder.arrived(g, k)

            def body(i):
                j = k * remainder.chunk + i
                t = g * 32 + 2 * j
                first = jnp.concatenate([corner.total(g, j), strip.total(g, j)], axis=0)
                more = remainder.total(g, j)
                mixed = more[:96]
                upper, lower = pl.ds(0, 96), pl.ds(96, 32)
                out_ref[t, upper] += jnp.where(low, first, mixed)
                out_ref[t, lower] += more[96:128]
                out_ref[t + 1, upper] += pltpu.roll(jnp.where(low, mixed, first), HALF, 1)
                out_ref[t + 1, lower] += more[128:]

            each(remainder.chunk, body, 4)

        loop(2, group)

    loop(remainder.parts, finish)

    remainder.near_sent()


def on_device(x_tiles, x_cols, c_list, c_count):
    hbm = pl.BlockSpec(memory_space=pltpu.HBM)
    dma = pltpu.SemaphoreType.DMA
    bf16 = lambda *dims: pltpu.VMEM(dims + (EDGE,), jnp.bfloat16)
    ints = lambda *dims: pltpu.VMEM(dims, jnp.int32)
    buffers = lambda n: [bf16(2, PAIRS, n), bf16(2, PAIRS, n), bf16(2, 2, PAIRS, n), bf16(2, 2, PAIRS, n)]
    semaphores = lambda n: [dma((2, n)), dma((2, n)), dma((2, 2, n)), dma((2, 2, n))]
    operands = [
        pltpu.with_memory_space_constraint(v, pltpu.HBM)
        for v in (x_tiles.reshape(16, EDGE, EDGE), jnp.swapaxes(x_cols, 1, 2),
                  jnp.swapaxes(c_list[0, 0], 0, 1))
    ]
    out = pl.pallas_call(
        kernel,
        out_shape=pltpu.VMEM((64, EDGE, EDGE), jnp.float32),
        in_specs=[hbm] * 3 + [pl.BlockSpec(memory_space=pltpu.SMEM)],
        out_specs=pl.BlockSpec(memory_space=pltpu.VMEM),
        scratch_shapes=[
            *[bf16(A_UNITS, n) for n in ROWS], *[bf16(B_UNITS, n) for n in ROWS],
            buffers(64), buffers(32), buffers(160),
            ints(2, 8, 8, EDGE), ints(4, 8, EDGE),
            pltpu.SMEM((2, 2, 4), jnp.int32), ints(2, 256),
            ints(8, 256), pltpu.SMEM((8, 256), jnp.int32),
            dma((3, 2)), dma((3,)), dma((108,)), dma((3, 16, 2)), dma((3, 4, 2)),
            dma((11,)), dma((9,)), dma((4,)),
            semaphores(Q_PARTS), semaphores(S_PARTS), semaphores(R_PARTS),
        ],
        compiler_params=pltpu.CompilerParams(
            collective_id=0, has_side_effects=True, vmem_limit_bytes=40 * 1024 * 1024),
    )(*operands, c_count)
    return out[None, None]


def solution(mesh):
    return jax.shard_map(
        on_device,
        mesh=mesh,
        in_specs=(
            P("layer", ("row", "col"), None, None, None),
            P("layer", ("row", "col"), None),
            P("row", "col", None, None),
            P("row", "col"),
        ),
        out_specs=P("row", "col", "layer", None, None),
        check_vma=False,
    )
```
